32 devices in a mesh: dp: 8 (over y, x, core), tensor: 4 (over z).
Axes of the slice: x: 2, y: 2, z: 4, core: 2. Of those that a mesh axis runs over, the one named last changes fastest.
Arguments:
- hidden_in: bfloat16 [8192, 1024], P(('dp', 'tensor')), may hold values from -6 to 6
- out_grad: bfloat16 [8192, 1024], P(('dp', 'tensor')), may hold values from -6 to 6
- positions: int32 [8192], P('dp'), may hold values from 0 to 1023, as said below
- query_weight: float32 [1024, 2048], P('dp', 'tensor'), may hold values from -0.1875 to 0.1875
- key_matrix: float32 [1024, 1024], P('dp', 'tensor'), may hold values from -0.1875 to 0.1875
- value_matrix: float32 [1024, 1024], P('dp', 'tensor'), may hold values from -0.1875 to 0.1875
- out_weight: float32 [2048, 1024], P('tensor', 'dp'), may hold values from -1 to 1
- gate_weight: float32 [1024, 3072], P('dp', 'tensor'), may hold values from -0.1875 to 0.1875
- up_weight: float32 [1024, 3072], P('dp', 'tensor'), may hold values from -0.1875 to 0.1875
- down_weight: float32 [3072, 1024], P('tensor', 'dp'), may hold values from -0.109375 to 0.109375
- query_moment: float32 [1024, 2048], P('dp', 'tensor'), may hold values from -814.58701 to 814.58701, as said below
- key_momentum: float32 [1024, 1024], P('dp', 'tensor'), may hold values from -814.58701 to 814.58701, as said below
- value_momentum: float32 [1024, 1024], P('dp', 'tensor'), may hold values from -1629.17402 to 1629.17402, as said below
- out_moment: float32 [2048, 1024], P('tensor', 'dp'), may hold values from -488.7522 to 488.7522, as said below
- gate_moment: float32 [1024, 3072], P('dp', 'tensor'), may hold values from -977.5044 to 977.5044, as said below
- up_moment: float32 [1024, 3072], P('dp', 'tensor'), may hold values from -977.5044 to 977.5044, as said below
- down_moment: float32 [3072, 1024], P('tensor', 'dp'), may hold values from -977.5044 to 977.5044, as said below
- gains: float32 [2304], replicated, may hold values from 0.5 to 1.5
- gain_first: float32 [2304], replicated, may hold values from -64 to 64
- gain_second: float32 [2304], replicated, may hold values from 212.992 to 3440.64
Outputs:
- block_out: float32 [8192, 1024], P(('dp', 'tensor'))
- input_grad: float32 [8192, 1024], P(('dp', 'tensor'))
- query_grad: float32 [1024, 2048], P('dp', 'tensor')
- key_grad: float32 [1024, 1024], P('dp', 'tensor')
- value_grad: float32 [1024, 1024], P('dp', 'tensor')
- out_weight_grad: float32 [2048, 1024], P('tensor', 'dp')
- gate_grad: float32 [1024, 3072], P('dp', 'tensor')
- up_grad: float32 [1024, 3072], P('dp', 'tensor')
- down_grad: float32 [3072, 1024], P('tensor', 'dp')
- query_new: float32 [1024, 2048], P('dp', 'tensor')
- key_new: float32 [1024, 1024], P('dp', 'tensor')
- value_new: float32 [1024, 1024], P('dp', 'tensor')
- out_weight_new: float32 [2048, 1024], P('tensor', 'dp')
- gate_new: float32 [1024, 3072], P('dp', 'tensor')
- up_new: float32 [1024, 3072], P('dp', 'tensor')
- down_new: float32 [3072, 1024], P('tensor', 'dp')
- query_moment_next: float32 [1024, 2048], P('dp', 'tensor')
- key_moment_next: float32 [1024, 1024], P('dp', 'tensor')
- value_moment_next: float32 [1024, 1024], P('dp', 'tensor')
- out_moment_next: float32 [2048, 1024], P('tensor', 'dp')
- gate_moment_next: float32 [1024, 3072], P('dp', 'tensor')
- up_moment_next: float32 [1024, 3072], P('dp', 'tensor')
- down_moment_next: float32 [3072, 1024], P('tensor', 'dp')
- gain_first_next: float32 [2304], replicated
- gain_second_next: float32 [2304], replicated
- gains_next: float32 [2304], replicated
The draws below stay inside these ranges and needn't reach their ends.
Inputs may be any that keep to these rules, and one draw needn't show every extreme that they name: `positions`: the 1024 tokens of one index of dp form one packed sequence of documents; a token's value is its distance from the first token of its document, so it is 0 where a document begins (always at the group's first token) and rises by one from token to token otherwise. In every group the first document begins at the first token and ends within the last 256 tokens. `query_moment`: momentum entries, of both signs. `key_momentum`: momentum entries, of both signs. `value_momentum`: momentum entries, of both signs. `out_moment`: momentum entries, of both signs. `gate_moment`: momentum entries, of both signs. `up_moment`: momentum entries, of both signs. `down_moment`: momentum entries, of both signs.
All inputs are finite; a program needn't handle non-finite values.
Results may differ from the reference program's by a relative error of at most 0.02.
Values may be sent and summed in bfloat16 or wider, within the bound.
No kernel may reach another device: no remote copies, remote signals or barrier semaphores. Data moves between devices by JAX's collectives and lax.ppermute only.
A program may use at most 128 MiB of HBM per device.

```python
import math
import jax
import jax.numpy as jnp
from jax import lax

MODEL_WIDTH = 1024
QUERY_HEADS = 16
KEY_VALUE_HEADS = 8
HEAD_SIZE = 128
FF = 3072
TOK_DEV = 256
DOC_LEN = 1024
NS_STEPS = 5
ADAM_STEP = 10
TOK_DP = 1024
TOKEN_TOTAL = 8192
N_TENSOR = 4


def draw_positions(key, part):
    key = jax.random.fold_in(key, 11)
    key_begins, key_ends, key_whole = jax.random.split(key, 3)
    group_count = TOKEN_TOTAL // TOK_DP
    index_row = jnp.arange(TOK_DP, dtype=jnp.int32)
    begins = jax.random.randint(key_begins, (group_count, TOK_DP), 0, DOC_LEN) == 0
    ends = jax.random.randint(key_ends, (group_count,), TOK_DP - TOK_DEV + 1, TOK_DP + 1)
    whole_group = jax.random.randint(key_whole, (), 0, group_count)
    ends = jnp.where(jnp.arange(group_count, dtype=jnp.int32) == whole_group, TOK_DP, ends)
    inside = index_row[None, :] < ends[:, None]
    begins = jnp.where(inside, index_row[None, :] == 0, begins | (index_row[None, :] == ends[:, None]))
    marks = jnp.where(begins, index_row[None, :], 0)
    return (index_row[None, :] - lax.cummax(marks, axis=1)).reshape(TOKEN_TOTAL).astype(jnp.int32)


def momentum_draw(key, row_count, col_count, entry_scale, transposed):
    key_noise, key_rows, key_cols, key_block = jax.random.split(key, 4)
    noise_part = jnp.clip(jax.random.normal(key_noise, (row_count, col_count), jnp.float32), -6.0, 6.0)
    row_signs = (jax.random.randint(key_rows, (row_count,), 0, 2) * 2 - 1).astype(jnp.float32)
    column_factor = jnp.clip(jax.random.normal(key_cols, (col_count,), jnp.float32), -3.0, 3.0)
    block_width = col_count // N_TENSOR
    chosen = jax.random.randint(key_block, (), 0, N_TENSOR)
    inside = jnp.arange(col_count, dtype=jnp.int32) // block_width == chosen
    strength = 2.0 * math.sqrt(N_TENSOR)
    column_part = jnp.where(inside, column_factor, 0.0)
    moment_draw = (noise_part + strength * row_signs[:, None] * column_part[None, :]) * entry_scale
    return moment_draw.T if transposed else moment_draw


def draw_query_moment(key, part):
    key = jax.random.fold_in(key, 21)
    return momentum_draw(key, MODEL_WIDTH, QUERY_HEADS * HEAD_SIZE, 0.5 * TOKEN_TOTAL ** 0.5, False)


def draw_key_momentum(key, part):
    key = jax.random.fold_in(key, 22)
    return momentum_draw(key, MODEL_WIDTH, KEY_VALUE_HEADS * HEAD_SIZE, 0.5 * TOKEN_TOTAL ** 0.5, False)


def draw_value_momentum(key, part):
    key = jax.random.fold_in(key, 23)
    return momentum_draw(key, MODEL_WIDTH, KEY_VALUE_HEADS * HEAD_SIZE, TOKEN_TOTAL ** 0.5, False)


def draw_out_moment(key, part):
    key = jax.random.fold_in(key, 24)
    return momentum_draw(key, MODEL_WIDTH, QUERY_HEADS * HEAD_SIZE, 0.3 * TOKEN_TOTAL ** 0.5, True)


def draw_gate_moment(key, part):
    key = jax.random.fold_in(key, 25)
    return momentum_draw(key, MODEL_WIDTH, FF, 0.6 * TOKEN_TOTAL ** 0.5, False)


def draw_up_moment(key, part):
    key = jax.random.fold_in(key, 26)
    return momentum_draw(key, MODEL_WIDTH, FF, 0.6 * TOKEN_TOTAL ** 0.5, False)


def draw_down_moment(key, part):
    key = jax.random.fold_in(key, 27)
    return momentum_draw(key, MODEL_WIDTH, FF, 0.6 * TOKEN_TOTAL ** 0.5, True)


def block_levels(stream_key, dims, shards, smallest, largest):
    loudness = 1.0
    for axis_at, parts in shards:
        steps = jax.random.uniform(jax.random.fold_in(jax.random.fold_in(stream_key, 6), axis_at), (parts,), jnp.float32, smallest / len(shards), largest / len(shards))
        loudness = loudness * jnp.repeat(jnp.exp(steps), dims[axis_at] // parts).reshape((-1,) + (1,) * (len(dims) - 1 - axis_at))
    return loudness


def noise(own_key, shape, scale, most, pieces=(), kind=jnp.bfloat16):
    level = block_levels(own_key, shape, pieces, -0.22, 0.18) if pieces else 1.0
    values = jax.random.normal(own_key, shape, jnp.float32) * scale * level
    return jnp.minimum(jnp.maximum(values, -most), most).astype(kind)


def setup_inputs(seed: int = 0) -> dict:
    arg_keys = jax.random.split(jax.random.key(seed), 21)
    return {
        "hidden_in": noise(arg_keys[0], (TOKEN_TOTAL, MODEL_WIDTH), 1.0, 6.0, ((0, 32),)),
        "out_grad": noise(arg_keys[1], (TOKEN_TOTAL, MODEL_WIDTH), 1.0, 6.0, ((0, 32),)),
        "positions": draw_positions(jax.random.fold_in(arg_keys[20], 71), 0),
        "query_weight": noise(arg_keys[3], (MODEL_WIDTH, QUERY_HEADS * HEAD_SIZE), MODEL_WIDTH ** -0.5, 0.1875, ((0, 8), (1, 4)), jnp.float32),
        "key_matrix": noise(arg_keys[4], (MODEL_WIDTH, KEY_VALUE_HEADS * HEAD_SIZE), MODEL_WIDTH ** -0.5, 0.1875, ((0, 8), (1, 4)), jnp.float32),
        "value_matrix": noise(arg_keys[5], (MODEL_WIDTH, KEY_VALUE_HEADS * HEAD_SIZE), MODEL_WIDTH ** -0.5, 0.1875, ((0, 8), (1, 4)), jnp.float32),
        "out_weight": noise(arg_keys[6], (QUERY_HEADS * HEAD_SIZE, MODEL_WIDTH), (QUERY_HEADS * HEAD_SIZE // 64) ** -0.5, 1.0, ((0, 4), (1, 8)), jnp.float32),
        "gate_weight": noise(arg_keys[7], (MODEL_WIDTH, FF), MODEL_WIDTH ** -0.5, 0.1875, ((0, 8), (1, 4)), jnp.float32),
        "up_weight": noise(arg_keys[8], (MODEL_WIDTH, FF), MODEL_WIDTH ** -0.5, 0.1875, ((0, 8), (1, 4)), jnp.float32),
        "down_weight": noise(arg_keys[9], (FF, MODEL_WIDTH), FF ** -0.5, 0.109375, ((0, 4), (1, 8)), jnp.float32),
        "query_moment": draw_query_moment(jax.random.fold_in(arg_keys[20], 71), 0),
        "key_momentum": draw_key_momentum(jax.random.fold_in(arg_keys[20], 71), 0),
        "value_momentum": draw_value_momentum(jax.random.fold_in(arg_keys[20], 71), 0),
        "out_moment": draw_out_moment(jax.random.fold_in(arg_keys[20], 71), 0),
        "gate_moment": draw_gate_moment(jax.random.fold_in(arg_keys[20], 71), 0),
        "up_moment": draw_up_moment(jax.random.fold_in(arg_keys[20], 71), 0),
        "down_moment": draw_down_moment(jax.random.fold_in(arg_keys[20], 71), 0),
        "gains": jnp.clip(1.0 + 0.1 * jax.random.normal(arg_keys[17], (2 * MODEL_WIDTH + 2 * HEAD_SIZE,), jnp.float32), 0.5, 1.5),
        "gain_first": noise(arg_keys[18], (2 * MODEL_WIDTH + 2 * HEAD_SIZE,), (0.11 * TOKEN_TOTAL ** 0.5), 64.0, (), jnp.float32),
        "gain_second": jnp.clip(jnp.exp(jax.random.uniform(arg_keys[19], (2 * MODEL_WIDTH + 2 * HEAD_SIZE,), jnp.float32, math.log(212.992), math.log(3440.64))), 212.992, 3440.64),
    }


EPS_NORM = 1e-06
ROPE_BASE = 1000000.0
MASK_FILL = -1e+30
MOMENTUM = 0.95
COEF_LINEAR = 3.4445
COEF_GRAM = -4.775
COEF_SQUARE = 2.0315
NS_EPS = 1e-07
DECAY_KEEP = 0.998
BETA_FIRST = 0.9
BETA_SECOND = 0.95
ADAM_EPS = 1e-08
GAIN_RATE = 0.6
HIGHEST = lax.Precision.HIGHEST

@jax.custom_vjp
def lowered_input(v):
    return lax.optimization_barrier(v.astype(jnp.bfloat16)).astype(jnp.float32)

@jax.custom_vjp
def lowered_cotangent(v):
    return v

def low_keep(v):
    return (lowered_input(v), None)

def low_pass(kept, grad):
    return (grad,)

def back_keep(v):
    return (v, None)

def back_low(kept, grad):
    return (lowered_input(grad),)
lowered_input.defvjp(low_keep, low_pass)
lowered_cotangent.defvjp(back_keep, back_low)

def matrix_product(left, right):
    return jnp.dot(left, right, preferred_element_type=jnp.float32, precision=HIGHEST)

def gram_of(matrix):
    return lax.dot_general(matrix, matrix, (((1,), (1,)), ((), ())), preferred_element_type=jnp.float32, precision=HIGHEST)

def rms_norm(values, gain):
    return values * lax.rsqrt(lax.optimization_barrier(jnp.mean(values * values, axis=-1, keepdims=True)) + EPS_NORM) * gain

def rotary(positions):
    half_width = HEAD_SIZE // 2
    inverse = jnp.power(jnp.float32(ROPE_BASE), -(jnp.arange(half_width, dtype=jnp.float32) * (2.0 / HEAD_SIZE)))
    angles = positions.astype(jnp.float32)[:, None] * inverse[None, :]
    cosine_part = jnp.cos(angles)
    sine_part = jnp.sin(angles)
    return (jnp.concatenate([cosine_part, cosine_part], axis=-1), jnp.concatenate([sine_part, sine_part], axis=-1))

def rotate(values, cosine_part, sine_part):
    half_width = values.shape[-1] // 2
    turned = jnp.concatenate([-values[..., half_width:], values[..., :half_width]], axis=-1)
    return values * cosine_part[:, None, :] + turned * sine_part[:, None, :]

def attend_block(query_block, first_row, pos_block, key_heads, value_heads):
    score_scale = HEAD_SIZE ** (-0.5)
    scores = lowered_cotangent(jnp.einsum('qhgd,khd->hgqk', query_block, key_heads, precision=HIGHEST) * score_scale)
    row_ids = first_row + jnp.arange(query_block.shape[0], dtype=jnp.int32)
    col_ids = jnp.arange(key_heads.shape[0], dtype=jnp.int32)
    visible = (col_ids[None, :] <= row_ids[:, None]) & (row_ids[:, None] - col_ids[None, :] <= pos_block[:, None])
    masked = jnp.where(visible[None, None], scores, MASK_FILL)
    row_max = lax.optimization_barrier(jnp.max(masked, axis=-1, keepdims=True))
    log_total = row_max + jnp.log(lax.optimization_barrier(jnp.sum(jnp.exp(masked - row_max), axis=-1, keepdims=True)))
    weights = lowered_input(jnp.exp(masked - log_total))
    return jnp.einsum('hgqk,khd->qhgd', weights, value_heads, precision=HIGHEST)

def layer(params, rows_in, positions):
    query_weight, key_matrix, value_matrix, out_weight, gate_weight, up_weight, down_weight, gains = params
    gain_attn = gains[:MODEL_WIDTH]
    gain_mlp = gains[MODEL_WIDTH:2 * MODEL_WIDTH]
    gain_query = gains[2 * MODEL_WIDTH:2 * MODEL_WIDTH + HEAD_SIZE]
    gain_key = gains[2 * MODEL_WIDTH + HEAD_SIZE:]
    total_rows = rows_in.shape[0]
    cosine_part, sine_part = rotary(positions)
    normalized = lowered_input(rms_norm(rows_in, gain_attn))
    query_pre = lowered_cotangent(matrix_product(normalized, lowered_input(query_weight))).reshape(total_rows, QUERY_HEADS, HEAD_SIZE)
    key_before_rotary = lowered_cotangent(matrix_product(normalized, lowered_input(key_matrix))).reshape(total_rows, KEY_VALUE_HEADS, HEAD_SIZE)
    value_before_heads = lowered_cotangent(matrix_product(normalized, lowered_input(value_matrix))).reshape(total_rows, KEY_VALUE_HEADS, HEAD_SIZE)
    query_head_rows = lowered_input(rotate(rms_norm(query_pre, gain_query), cosine_part, sine_part))
    key_heads = lowered_input(rotate(rms_norm(key_before_rotary, gain_key), cosine_part, sine_part))
    value_heads = lowered_input(value_before_heads)
    rows_per_block = min(512, total_rows)
    block_number = total_rows // rows_per_block
    query_block_list = query_head_rows.reshape(block_number, rows_per_block, KEY_VALUE_HEADS, QUERY_HEADS // KEY_VALUE_HEADS, HEAD_SIZE)
    first_rows = jnp.arange(block_number, dtype=jnp.int32) * rows_per_block
    pos_blocks = positions.reshape(block_number, rows_per_block)

    def one_block(inputs):
        query_block, first_row, pos_block = inputs
        return attend_block(query_block, first_row, pos_block, key_heads, value_heads)
    mixed_blocks = lax.map(jax.checkpoint(one_block), (query_block_list, first_rows, pos_blocks))
    mixed = lowered_input(lowered_cotangent(mixed_blocks.reshape(total_rows, QUERY_HEADS * HEAD_SIZE)))
    residual = rows_in + lowered_cotangent(matrix_product(mixed, lowered_input(out_weight)))
    normed_mlp = lowered_input(rms_norm(residual, gain_mlp))
    gate_value = lowered_cotangent(matrix_product(normed_mlp, lowered_input(gate_weight)))
    up_value = lowered_cotangent(matrix_product(normed_mlp, lowered_input(up_weight)))
    activated = lowered_input(jax.nn.silu(gate_value) * up_value)
    return residual + lowered_cotangent(matrix_product(activated, lowered_input(down_weight)))

def orthogonalize(matrix):
    current = matrix / (jnp.sqrt(jnp.sum(matrix * matrix)) + NS_EPS)
    for sweep_number in range(NS_STEPS):
        gram_matrix = gram_of(current)
        mixture = COEF_GRAM * gram_matrix + COEF_SQUARE * matrix_product(gram_matrix, gram_matrix)
        current = COEF_LINEAR * current + matrix_product(mixture, current)
    return current

def reference(hidden_in, out_grad, positions, query_weight, key_matrix, value_matrix, out_weight, gate_weight, up_weight, down_weight, query_moment, key_momentum, value_momentum, out_moment, gate_moment, up_moment, down_moment, gains, gain_first, gain_second):
    masters = (query_weight, key_matrix, value_matrix, out_weight, gate_weight, up_weight, down_weight)
    moments = (query_moment, key_momentum, value_momentum, out_moment, gate_moment, up_moment, down_moment)
    params = masters + (gains,)
    group_count = TOKEN_TOTAL // TOK_DP
    inputs_all = hidden_in.astype(jnp.float32).reshape(group_count, TOK_DP, MODEL_WIDTH)
    cotangents = out_grad.astype(jnp.float32).reshape(group_count, TOK_DP, MODEL_WIDTH)
    pos_all = positions.reshape(group_count, TOK_DP)

    def group_step(totals, items):
        rows_in, cotangent, pos_rows = items

        def run(param_set, rows_value):
            return layer(param_set, rows_value, pos_rows)
        rows_out, pull = jax.vjp(run, params, rows_in)
        param_grads, rows_grad = pull(cotangent)
        return (jax.tree.map(jnp.add, totals, param_grads), (rows_out, rows_grad))
    zeros = jax.tree.map(jnp.zeros_like, params)
    grads, (outputs, input_grads) = lax.scan(group_step, zeros, (inputs_all, cotangents, pos_all))
    flipped = (False, False, False, True, False, False, True)
    fans = (MODEL_WIDTH, MODEL_WIDTH, MODEL_WIDTH, QUERY_HEADS * HEAD_SIZE // 64, MODEL_WIDTH, MODEL_WIDTH, FF)
    news = []
    nexts = []
    for number in range(7):
        moment_next = MOMENTUM * moments[number] + grads[number]
        looked = grads[number] + MOMENTUM * moment_next
        oriented = looked.T if flipped[number] else looked
        ortho = orthogonalize(oriented)
        if flipped[number]:
            ortho = ortho.T
        step_size = 0.5 * fans[number] ** (-0.5) * math.sqrt(max(masters[number].shape))
        news.append(DECAY_KEEP * masters[number] - step_size * ortho)
        nexts.append(moment_next)
    gain_grad = grads[7]
    first_next = BETA_FIRST * gain_first + (1.0 - BETA_FIRST) * gain_grad
    second_next = BETA_SECOND * gain_second + (1.0 - BETA_SECOND) * gain_grad * gain_grad
    first_hat = first_next / (1.0 - BETA_FIRST ** ADAM_STEP)
    second_hat = second_next / (1.0 - BETA_SECOND ** ADAM_STEP)
    gains_next = gains - GAIN_RATE * first_hat / (jnp.sqrt(second_hat) + ADAM_EPS)
    return (outputs.reshape(TOKEN_TOTAL, MODEL_WIDTH), input_grads.reshape(TOKEN_TOTAL, MODEL_WIDTH), grads[0], grads[1], grads[2], grads[3], grads[4], grads[5], grads[6], news[0], news[1], news[2], news[3], news[4], news[5], news[6], nexts[0], nexts[1], nexts[2], nexts[3], nexts[4], nexts[5], nexts[6], first_next, second_next, gains_next)
```

```python
import functools
import math

import jax
import jax.numpy as jnp
from jax import lax
from jax.experimental import pallas as pl
from jax.experimental.pallas import tpu as pltpu
from jax.sharding import Mesh, PartitionSpec as P

MODEL_WIDTH = 1024
QUERY_HEADS = 16
KEY_VALUE_HEADS = 8
HEAD_SIZE = 128
FF = 3072
NS_STEPS = 5
ADAM_STEP = 10


EPS_NORM = 1e-06
ROPE_BASE = 1000000.0
MASK_FILL = -1e30
MOMENTUM = 0.95
COEF_LINEAR = 3.4445
COEF_GRAM = -4.775
COEF_SQUARE = 2.0315
NS_EPS = 1e-07
DECAY_KEEP = 0.998
BETA_FIRST = 0.9
BETA_SECOND = 0.95
ADAM_EPS = 1e-08
GAIN_RATE = 0.6
ROW_BLOCK = 256


DP = ("pl", "core")
TENSOR = ("hi", "lo")


def matmul(left, right):
    return jnp.dot(left, right, preferred_element_type=jnp.float32)


def contract_rows(left, right):
    return lax.dot_general(
        left, right, (((0,), (0,)), ((), ())), preferred_element_type=jnp.float32
    )


def contract_cols(left, right):
    return lax.dot_general(
        left, right, (((1,), (1,)), ((), ())), preferred_element_type=jnp.float32
    )


def orthogonalize_kernel(owner_ref, *refs):
    count = (len(refs) - 4) // 2

    @pl.when(owner_ref[0] != 0)
    def _():
        orthogonalize_owned(count, refs)

    @pl.when(owner_ref[0] == 0)
    def _():
        for result in refs[count : 2 * count]:
            result[...] = jnp.zeros_like(result)


def orthogonalize_owned(count, refs):
    pieces, results = refs[:count], refs[count : 2 * count]
    current, gram, gram_low, mixing = refs[2 * count :]
    size, width = pieces[0].shape
    block = 256
    blocks = size // block
    for number, piece in enumerate(pieces):
        current[:, number * width : (number + 1) * width] = piece[...]
    diagonal = lax.broadcasted_iota(jnp.int32, (block, block), 0) == lax.broadcasted_iota(
        jnp.int32, (block, block), 1
    )

    def mix(number):
        for col in range(blocks):
            at = col * block
            gram[at:, at : at + block] = contract_cols(current[at:, :], current[at : at + block, :])
        trace = jnp.float32(0.0)
        for col in range(blocks):
            at = col * block
            trace += jnp.sum(jnp.where(diagonal, gram[at : at + block, at : at + block], 0.0))
        scale = jnp.where(number == 0, 1.0 / (jnp.sqrt(trace) + NS_EPS), 1.0)
        scale_square = scale * scale
        for col in range(blocks):
            at = col * block
            for row in range(col, blocks):
                to = row * block
                tile = gram[to : to + block, at : at + block] * scale_square
                gram[to : to + block, at : at + block] = tile
                gram_low[to : to + block, at : at + block] = tile.astype(jnp.bfloat16)
                if row > col:
                    gram_low[at : at + block, to : to + block] = tile.T.astype(jnp.bfloat16)
        for col in range(blocks):
            at = col * block
            square = matmul(gram_low[at:, :], gram_low[:, at : at + block])
            for row in range(col, blocks):
                to = row * block
                tile = COEF_GRAM * gram[to : to + block, at : at + block]
                tile += COEF_SQUARE * square[to - at : to - at + block]
                if row == col:
                    tile += jnp.where(diagonal, COEF_LINEAR, 0.0)
                tile = tile * scale
                mixing[to : to + block, at : at + block] = tile.astype(jnp.bfloat16)
                if row > col:
                    mixing[at : at + block, to : to + block] = tile.T.astype(jnp.bfloat16)

    def sweep(number, carry):
        mix(number)

        def columns(step, inner):
            span = pl.ds(pl.multiple_of(step * width, width), width)
            current[:, span] = matmul(mixing[...], current[:, span]).astype(jnp.bfloat16)
            return inner

        lax.fori_loop(0, count, columns, 0)
        return carry

    lax.fori_loop(0, NS_STEPS, sweep, 0)
    for number, result in enumerate(results):
        result[...] = current[:, number * width : (number + 1) * width]


def orthogonalize(owner, pieces):
    size, width = pieces[0].shape
    total = width * len(pieces)
    flops = NS_STEPS * 2 * size * size * (total * 13 // 8 + size * 5 // 8)
    return pl.pallas_call(
        orthogonalize_kernel,
        out_shape=[jax.ShapeDtypeStruct(piece.shape, piece.dtype) for piece in pieces],
        in_specs=[pl.BlockSpec(memory_space=pltpu.SMEM)]
        + [pl.BlockSpec(memory_space=pltpu.VMEM)] * len(pieces),
        out_specs=[pl.BlockSpec(memory_space=pltpu.VMEM)] * len(pieces),
        scratch_shapes=[
            pltpu.VMEM((size, total), jnp.bfloat16),
            pltpu.VMEM((size, size), jnp.float32),
            pltpu.VMEM((size, size), jnp.bfloat16),
            pltpu.VMEM((size, size), jnp.bfloat16),
        ],
        compiler_params=pltpu.CompilerParams(vmem_limit_bytes=48 * 1024 * 1024),
        cost_estimate=pl.CostEstimate(
            flops=flops, bytes_accessed=4 * size * total, transcendentals=0
        ),
    )(owner.astype(jnp.int32).reshape(1), *pieces)


def tied(*values):
    return lax.optimization_barrier(values)


def swap(values):
    return lax.ppermute(values, ("core", "hi"), [(0, 0), (1, 2), (2, 1), (3, 3)])


def to_partner(values, name):
    return lax.ppermute(values, name, [(0, 1), (1, 0)])


def in_order(first, mine, theirs):
    return jnp.concatenate([jnp.where(first, mine, theirs), jnp.where(first, theirs, mine)], axis=0)


def half_of(values, which):
    rows = values.shape[0] // 2
    return lax.dynamic_slice_in_dim(values, which * rows, rows, 0)


def gather_near(values, ordered):
    if lax.axis_size("lo") == 2:
        other = to_partner(values, "lo")
        if ordered:
            return in_order(lax.axis_index("lo") == 0, values, other)
        return jnp.concatenate([values, other], axis=0)
    return lax.all_gather(values, "lo", axis=0, tiled=True)


def gather_across(pair, ordered):
    other = to_partner(pair, "core")
    if ordered:
        return in_order(lax.axis_index("core") == 0, pair, other)
    return jnp.concatenate([pair, other], axis=0)


def scatter_across(values, ordered):
    place = lax.axis_index("core") if ordered else 0
    received = to_partner(half_of(values, 1 - place), "core").astype(jnp.float32)
    return half_of(values, place).astype(jnp.float32) + received


def scatter_near(pair, ordered):
    if lax.axis_size("lo") == 2:
        place = lax.axis_index("lo") if ordered else 0
        received = to_partner(half_of(pair, 1 - place).astype(jnp.bfloat16), "lo")
        return half_of(pair, place) + received.astype(jnp.float32)
    return lax.psum_scatter(
        pair.astype(jnp.bfloat16), "lo", scatter_dimension=0, tiled=True
    ).astype(jnp.float32)


def scatter_tokens(values, ordered):
    return scatter_near(scatter_across(values, ordered), ordered)


def both_cores(shard):
    return in_order(lax.axis_index("core") == 0, shard, to_partner(shard, "core"))


def exchange(values, stride):
    count = lax.axis_size("pl")
    return lax.ppermute(values, "pl", [(index, index ^ stride) for index in range(count)])


def in_places(found, held):
    rows = held.shape[0] * lax.axis_size("pl")
    full = jnp.zeros((rows, held.shape[1]), held.dtype)
    for piece, at in found:
        full = lax.dynamic_update_slice_in_dim(full, piece, at, 0)
    return full


def gather_plane_direct(held):
    place = lax.axis_index("pl")
    rows = held.shape[0]
    found = [(held, place * rows)]
    for stride in range(1, lax.axis_size("pl")):
        found.append((exchange(held, stride), (place ^ stride) * rows))
    return in_places(found, held)


def gather_plane_near(held):
    if lax.axis_size("pl") != 4:
        return [held] + [exchange(held, stride) for stride in range(1, lax.axis_size("pl"))]
    return [held, exchange(held, 1), exchange(held, 2)]


def gather_plane_far(near):
    place = lax.axis_index("pl")
    rows = near[0].shape[0]
    half = rows // 2
    found = [(piece, (place ^ stride) * rows) for stride, piece in enumerate(near)]
    if lax.axis_size("pl") == 4:
        found.append((exchange(near[2][:half], 1), (place ^ 3) * rows))
        found.append((exchange(near[1][half:], 2), (place ^ 3) * rows + half))
    return in_places(found, near[0])


def gather_plane(held):
    return gather_plane_far(gather_plane_near(held))


def sum_far(values):
    count = lax.axis_size("pl")
    place = lax.axis_index("pl")
    rows = values.shape[0] // count
    half = rows // 2
    chunks = [
        lax.dynamic_slice_in_dim(values, (place ^ stride) * rows, rows, 0) for stride in range(count)
    ]
    if count != 4:
        return chunks
    return chunks[:3] + [exchange(chunks[3][half:], 2), exchange(chunks[3][:half], 1)]


def sum_near(chunks):
    count = lax.axis_size("pl")
    if count != 4:
        return chunks[:1] + [exchange(chunks[stride], stride) for stride in range(1, count)]
    mine, first, second, for_first, for_second = chunks
    half = mine.shape[0] // 2
    first = jnp.concatenate([first[:half], add(first[half:], for_first)], axis=0)
    second = jnp.concatenate([add(second[:half], for_second), second[half:]], axis=0)
    return [mine, exchange(first, 1), exchange(second, 2)]


def sum_plane(values):
    return sum_near(sum_far(values))


def add(left, right):
    return (left.astype(jnp.float32) + right.astype(jnp.float32)).astype(jnp.bfloat16)


def cross_sum(pieces):
    total = sum(piece.astype(jnp.float32) for piece in pieces)
    return swap(total.astype(jnp.bfloat16))


def finish_sum(held):
    place = lax.axis_index("core")
    received = to_partner(half_of(held, 1 - place), "core")
    return half_of(held, place).astype(jnp.float32) + received.astype(jnp.float32)


def sum_everywhere(values, sizes):
    for name, count in sizes:
        stride = 1
        while stride < count:
            pairs = [(index, index ^ stride) for index in range(count)]
            values = values + lax.ppermute(values, name, pairs)
            stride *= 2
    return values


def rms_norm(values, gain):
    return values * lax.rsqrt(jnp.mean(values * values, axis=-1, keepdims=True) + EPS_NORM) * gain


def rotary(positions):
    half_width = HEAD_SIZE // 2
    inverse = jnp.power(
        jnp.float32(ROPE_BASE), -(jnp.arange(half_width, dtype=jnp.float32) * (2.0 / HEAD_SIZE))
    )
    angles = positions.astype(jnp.float32)[:, None] * inverse[None, :]
    cosine_part = jnp.cos(angles)
    sine_part = jnp.sin(angles)
    return (
        jnp.concatenate([cosine_part, cosine_part], axis=-1),
        jnp.concatenate([-sine_part, sine_part], axis=-1),
    )


def visible_pairs(start_ref, block, extent, rows):
    query = block * rows + lax.broadcasted_iota(jnp.int32, (extent, rows), 1)
    key = lax.broadcasted_iota(jnp.int32, (extent, rows), 0)
    begin = start_ref[:, block * rows : (block + 1) * rows]
    return (key <= query) & (key >= begin)


def turn_half(values):
    return pltpu.roll(values, HEAD_SIZE // 2, 1)


def project_kernel(
    rows_ref,
    weight_ref,
    cosine_ref,
    sine_ref,
    gain_query_ref,
    gain_key_ref,
    query_ref,
    key_ref,
    value_ref,
    pre_ref,
):
    total_rows = rows_ref.shape[0]
    width_query, width_key = query_ref.shape[1], key_ref.shape[1]
    size = ROW_BLOCK
    low = jnp.bfloat16

    def project(block, carry):
        span = pl.ds(pl.multiple_of(block * size, size), size)
        pre = matmul(rows_ref[span, :], weight_ref[...])
        pre_ref[span, :] = pre[:, : width_query + width_key]
        cosine, sine = cosine_ref[span, :], sine_ref[span, :]
        for at in range(0, width_query + width_key, HEAD_SIZE):
            gain_ref = gain_query_ref if at < width_query else gain_key_ref
            normal = rms_norm(pre[:, at : at + HEAD_SIZE], gain_ref[...])
            turned = (normal * cosine + turn_half(normal) * sine).astype(low)
            if at < width_query:
                query_ref[span, at : at + HEAD_SIZE] = turned
            else:
                key_ref[span, at - width_query : at - width_query + HEAD_SIZE] = turned
        value_ref[span, :] = pre[:, width_query + width_key :].astype(low)
        return carry

    lax.fori_loop(0, total_rows // size, project, 0)


def attend_kernel(
    query_ref, key_ref, value_ref, start_ref, mixed_ref, log_total_ref, turned_value
):
    total_rows = query_ref.shape[0]
    width_query, width_key = query_ref.shape[1], key_ref.shape[1]
    size = ROW_BLOCK
    scale = HEAD_SIZE**-0.5
    low = jnp.bfloat16

    def prepare(block, carry):
        span = pl.ds(pl.multiple_of(block * size, size), size)
        for at in range(0, width_key, HEAD_SIZE):
            value = value_ref[span, at : at + HEAD_SIZE].astype(jnp.float32)
            turned_value[at : at + HEAD_SIZE, span] = value.T.astype(low)
        return carry

    lax.fori_loop(0, total_rows // size, prepare, 0)
    group = width_query // width_key
    for block in range(total_rows // size):
        extent = (block + 1) * size
        rows = slice(block * size, extent)
        visible = visible_pairs(start_ref, block, extent, size)
        for head in range(width_query // HEAD_SIZE):
            key_at = head // group * HEAD_SIZE
            lanes = slice(head * HEAD_SIZE, (head + 1) * HEAD_SIZE)
            key_lanes = slice(key_at, key_at + HEAD_SIZE)
            scores = contract_cols(key_ref[:extent, key_lanes], query_ref[rows, lanes])
            scores = jnp.where(visible, scores, MASK_FILL)
            row_max = jnp.max(scores, axis=0, keepdims=True)
            weights = jnp.exp((scores - row_max) * scale)
            total = jnp.sum(weights, axis=0, keepdims=True)
            log_total_ref[head : head + 1, rows] = row_max * scale + jnp.log(total)
            weights = (weights * (1.0 / total)).astype(low)
            mixed = matmul(turned_value[key_lanes, :extent], weights)
            mixed_ref[rows, lanes] = mixed.T.astype(low)


def attention_backward_kernel(
    state_ref,
    out_ref,
    query_ref,
    key_ref,
    value_ref,
    pre_ref,
    log_total_ref,
    cosine_ref,
    sine_ref,
    gain_query_ref,
    gain_key_ref,
    start_ref,
    d_heads_ref,
    d_gain_ref,
    d_mixed,
    turned_key,
    d_query,
    d_key,
    d_value,
):
    total_rows = state_ref.shape[0]
    width_query, width_key = query_ref.shape[1], key_ref.shape[1]
    size = ROW_BLOCK
    scale = HEAD_SIZE**-0.5
    low = jnp.bfloat16

    def prepare(block, carry):
        span = pl.ds(pl.multiple_of(block * size, size), size)
        d_mixed[span, :] = matmul(state_ref[span, :], out_ref[...]).astype(low)
        for at in range(0, width_key, HEAD_SIZE):
            key = key_ref[span, at : at + HEAD_SIZE].astype(jnp.float32)
            turned_key[at : at + HEAD_SIZE, span] = key.T.astype(low)
        return carry

    lax.fori_loop(0, total_rows // size, prepare, 0)
    d_key[...] = jnp.zeros_like(d_key)
    d_value[...] = jnp.zeros_like(d_value)
    group = width_query // width_key
    for block in range(total_rows // size):
        extent = (block + 1) * size
        rows = slice(block * size, extent)
        visible = visible_pairs(start_ref, block, extent, size)
        for head in range(width_query // HEAD_SIZE):
            key_at = head // group * HEAD_SIZE
            lanes = slice(head * HEAD_SIZE, (head + 1) * HEAD_SIZE)
            key_lanes = slice(key_at, key_at + HEAD_SIZE)
            query = query_ref[rows, lanes]
            cotangent = d_mixed[rows, lanes]
            scores = contract_cols(key_ref[:extent, key_lanes], query) * scale
            probs = jnp.exp(scores - log_total_ref[head : head + 1, rows])
            probs = jnp.where(visible, probs, 0.0)
            d_probs = contract_cols(value_ref[:extent, key_lanes], cotangent)
            shift = jnp.sum(d_probs * probs, axis=0, keepdims=True)
            d_scores = (probs * (d_probs - shift)).astype(low)
            d_value[:extent, key_lanes] += matmul(probs.astype(low), cotangent)
            d_key[:extent, key_lanes] += matmul(d_scores, query)
            d_query[rows, lanes] = matmul(turned_key[key_lanes, :extent], d_scores).T * scale

    def finish(block, carry):
        span = pl.ds(pl.multiple_of(block * size, size), size)
        cosine, sine = cosine_ref[span, :], sine_ref[span, :]
        sums = []
        for at in range(0, width_query + width_key, HEAD_SIZE):
            if at < width_query:
                gain, cotangent = gain_query_ref[...], d_query[span, at : at + HEAD_SIZE]
            else:
                begin = at - width_query
                gain = gain_key_ref[...]
                cotangent = d_key[span, begin : begin + HEAD_SIZE] * scale
            cotangent = cotangent * cosine - turn_half(cotangent) * sine
            pre = pre_ref[span, at : at + HEAD_SIZE]
            inverse = lax.rsqrt(jnp.mean(pre * pre, axis=-1, keepdims=True) + EPS_NORM)
            normal = pre * inverse
            sums.append(jnp.sum(cotangent * normal, axis=0, keepdims=True))
            pulled = cotangent * gain
            inner = jnp.mean(normal * pulled, axis=-1, keepdims=True)
            d_pre = inverse * (pulled - normal * inner)
            d_heads_ref[span, at : at + HEAD_SIZE] = d_pre.astype(low)
        d_heads_ref[span, width_query + width_key :] = d_value[span, :].astype(low)
        heads_query = width_query // HEAD_SIZE
        return carry[0] + sum(sums[:heads_query]), carry[1] + sum(sums[heads_query:])

    zero = jnp.zeros((1, HEAD_SIZE), jnp.float32)
    for_query, for_key = lax.fori_loop(0, total_rows // size, finish, (zero, zero))
    d_gain_ref[0:1, :] = for_query
    d_gain_ref[1:2, :] = for_key


def in_vmem(kernel, operands, results, scratch, flops):
    moved = sum(math.prod(item.shape) * item.dtype.itemsize for item in operands + results)
    return pl.pallas_call(
        kernel,
        out_shape=results,
        in_specs=[pl.BlockSpec(memory_space=pltpu.VMEM)] * len(operands),
        out_specs=[pl.BlockSpec(memory_space=pltpu.VMEM)] * len(results),
        scratch_shapes=scratch,
        compiler_params=pltpu.CompilerParams(vmem_limit_bytes=48 * 1024 * 1024),
        cost_estimate=pl.CostEstimate(flops=flops, bytes_accessed=moved, transcendentals=0),
    )(*operands)


def project(rows, weight, cosine, sine, gain_query, gain_key, width_query):
    total_rows, columns = rows.shape
    width_key = (weight.shape[1] - width_query) // 2
    low = jnp.bfloat16
    shape = jax.ShapeDtypeStruct
    return in_vmem(
        project_kernel,
        [rows, weight, cosine, sine, gain_query, gain_key],
        [
            shape((total_rows, width_query), low),
            shape((total_rows, width_key), low),
            shape((total_rows, width_key), low),
            shape((total_rows, width_query + width_key), jnp.float32),
        ],
        [],
        2 * total_rows * columns * weight.shape[1],
    )


def attend(query, key, value, start):
    total_rows, width_query = query.shape
    width_key = key.shape[1]
    shape = jax.ShapeDtypeStruct
    return in_vmem(
        attend_kernel,
        [query, key, value, start],
        [
            shape((total_rows, width_query), jnp.bfloat16),
            shape((width_query // HEAD_SIZE, total_rows), jnp.float32),
        ],
        [pltpu.VMEM((width_key, total_rows), jnp.bfloat16)],
        4 * total_rows * total_rows * width_query,
    )


def attention_backward(
    state, out_full, saved, cosine, sine, gain_query, gain_key, start
):
    query, key, value, pre, log_total = saved
    total_rows, columns = state.shape
    width_query, width_key = query.shape[1], key.shape[1]
    low = jnp.bfloat16
    shape = jax.ShapeDtypeStruct
    return in_vmem(
        attention_backward_kernel,
        [state, out_full, query, key, value, pre, log_total]
        + [cosine, sine, gain_query, gain_key, start],
        [
            shape((total_rows, width_query + 2 * width_key), low),
            shape((2, HEAD_SIZE), jnp.float32),
        ],
        [
            pltpu.VMEM((total_rows, width_query), low),
            pltpu.VMEM((width_key, total_rows), low),
            pltpu.VMEM((total_rows, width_query), jnp.float32),
            pltpu.VMEM((total_rows, width_key), jnp.float32),
            pltpu.VMEM((total_rows, width_key), jnp.float32),
        ],
        2 * total_rows * columns * width_query + 10 * total_rows * total_rows * width_query,
    )


def home_row(index):
    return lax.axis_size(TENSOR) // 2 - 1 + index % 2


def owns(group, homes):
    index, row = lax.axis_index(DP), lax.axis_index(TENSOR)
    mine = functools.reduce(jnp.logical_or, [index == homes[number] for number in group])
    return mine & (row == home_row(index))


def toward_home(group, homes, step):
    rows = lax.axis_size(TENSOR)
    return [
        (index * rows + (home_row(index) + step) % rows, index * rows + home_row(index))
        for index in sorted(homes[number] for number in group)
    ]


def to_columns(slots):
    owned = lax.all_to_all(slots, DP, split_axis=0, concat_axis=0, tiled=True)
    return owned.reshape(-1, slots.shape[2])


def to_homes(group, homes, owned):
    return [owned] + [
        lax.ppermute(owned, DP + TENSOR, toward_home(group, homes, step))
        for step in range(1, lax.axis_size(TENSOR))
    ]


def from_homes(group, homes, back):
    index, row = lax.axis_index(DP), lax.axis_index(TENSOR)
    received = jnp.where(row == home_row(index), back[0], jnp.zeros_like(back[0]))
    for step in range(1, lax.axis_size(TENSOR)):
        pairs = [(target, source) for source, target in toward_home(group, homes, step)]
        received = received + lax.ppermute(back[step], DP + TENSOR, pairs)
    return received


def from_columns(received):
    shape = (lax.axis_size(DP), -1, received.shape[1])
    return lax.all_to_all(received.reshape(shape), DP, split_axis=0, concat_axis=0, tiled=True)


FLIPPED = (False, False, False, True, False, False, True)
SHAPES = (
    (MODEL_WIDTH, QUERY_HEADS * HEAD_SIZE),
    (MODEL_WIDTH, KEY_VALUE_HEADS * HEAD_SIZE),
    (MODEL_WIDTH, KEY_VALUE_HEADS * HEAD_SIZE),
    (QUERY_HEADS * HEAD_SIZE, MODEL_WIDTH),
    (MODEL_WIDTH, FF),
    (MODEL_WIDTH, FF),
    (FF, MODEL_WIDTH),
)
FANS = (
    MODEL_WIDTH,
    MODEL_WIDTH,
    MODEL_WIDTH,
    QUERY_HEADS * HEAD_SIZE // 64,
    MODEL_WIDTH,
    MODEL_WIDTH,
    FF,
)


def advance_kernel(homes, *refs):
    late_ref, out_ref, gate_up_ref, down_ref = refs[:4]
    moment_refs, reduced_refs, fresh_refs = refs[4:11], refs[11:18], refs[18:25]
    slots_ref = refs[25]
    width_query, width_key = moment_refs[0].shape[1], moment_refs[1].shape[1]
    width_ff = moment_refs[4].shape[1]
    gradients = (
        late_ref[:, :width_query],
        late_ref[:, width_query : width_query + width_key],
        late_ref[:, width_query + width_key :],
        out_ref[...],
        gate_up_ref[:, :width_ff],
        gate_up_ref[:, width_ff:],
        down_ref[...],
    )
    slots_ref[...] = jnp.zeros_like(slots_ref)
    for number, gradient in enumerate(gradients):
        moment = moment_refs[number][...]
        if FLIPPED[number]:
            gradient_turned = gradient.T
            moment_next = MOMENTUM * moment + gradient_turned
            reduced_refs[number][...] = gradient_turned
            look = (gradient_turned + MOMENTUM * moment_next).T
        else:
            moment_next = MOMENTUM * moment + gradient
            reduced_refs[number][...] = gradient
            look = gradient + MOMENTUM * moment_next
        fresh_refs[number][...] = moment_next
        slots_ref[homes[number], :, : look.shape[1]] = look.astype(jnp.bfloat16)


def advance(sums, moments, homes, dp_count):
    rows = sums[0].shape[0]
    width = max(moment.shape[1] for moment in moments)
    shapes = [jax.ShapeDtypeStruct(moment.shape, jnp.float32) for moment in moments]
    results = in_vmem(
        functools.partial(advance_kernel, homes),
        list(sums) + list(moments),
        shapes + shapes + [jax.ShapeDtypeStruct((dp_count, rows, width), jnp.bfloat16)],
        [],
        0,
    )
    return results[:7], results[7:14], results[14]


def update_kernel(homes, returned_ref, *refs):
    for number in range(7):
        master_ref, result_ref = refs[number], refs[7 + number]
        width = master_ref.shape[0] if FLIPPED[number] else master_ref.shape[1]
        portion = returned_ref[homes[number], :, :width].astype(jnp.float32)
        if FLIPPED[number]:
            portion = portion.T
        step_size = 0.5 * FANS[number] ** (-0.5) * math.sqrt(max(SHAPES[number]))
        result_ref[...] = DECAY_KEEP * master_ref[...] - step_size * portion


def update(returned, masters, homes):
    return in_vmem(
        functools.partial(update_kernel, homes),
        [returned] + list(masters),
        [jax.ShapeDtypeStruct(master.shape, jnp.float32) for master in masters],
        [],
        0,
    )


def on_device(
    hidden_in,
    out_grad,
    positions,
    query_weight,
    key_matrix,
    value_matrix,
    out_weight,
    gate_weight,
    up_weight,
    down_weight,
    query_moment,
    key_momentum,
    value_momentum,
    out_moment,
    gate_moment,
    up_moment,
    down_moment,
    gains,
    gain_first,
    gain_second,
):
    bf16 = jnp.bfloat16
    heads_local = jnp.concatenate(
        [query_weight.astype(bf16), key_matrix.astype(bf16), value_matrix.astype(bf16)], axis=1
    )
    out_local = out_weight.astype(bf16).T
    mlp_local = jnp.concatenate(
        [gate_weight.astype(bf16), up_weight.astype(bf16), down_weight.astype(bf16).T], axis=1
    )
    width_query = query_weight.shape[1]
    width_key = key_matrix.shape[1]
    width_ff = gate_weight.shape[1]
    heads_held = swap(both_cores(heads_local))
    hidden_in, positions, heads_held = tied(hidden_in, positions, heads_held)
    positions = swap(positions)
    hidden_in = swap(hidden_in)
    heads_near = gather_plane_near(heads_held)
    out_pair = both_cores(out_local)
    mlp_pair = both_cores(mlp_local)
    hidden_in, out_pair, heads_near = tied(hidden_in, out_pair, heads_near)
    heads_full = gather_plane_far(heads_near)
    out_held = swap(out_pair)
    gain_attn = gains[:MODEL_WIDTH]
    gain_mlp = gains[MODEL_WIDTH : 2 * MODEL_WIDTH]
    gain_query = gains[2 * MODEL_WIDTH : 2 * MODEL_WIDTH + HEAD_SIZE][None, :]
    gain_key = gains[2 * MODEL_WIDTH + HEAD_SIZE :][None, :]
    start = (jnp.arange(positions.shape[0], dtype=jnp.int32) - positions)[None, :]
    cosine_part, sine_part = rotary(positions)
    residual_in = hidden_in.astype(jnp.float32)
    normalized = rms_norm(residual_in, gain_attn).astype(jnp.bfloat16)

    attn_pair = gather_near(normalized, True)
    attn_pair, mlp_pair = tied(attn_pair, mlp_pair)
    mlp_held = swap(mlp_pair)
    attn_rows = gather_across(attn_pair, True)
    query, key, value, pre = project(
        attn_rows, heads_full, cosine_part, sine_part, gain_query, gain_key, width_query
    )
    query, out_held = tied(query, out_held)
    out_full = gather_plane_direct(out_held)
    mixed_heads, log_total = attend(query, key, value, start)
    mixed_heads, mlp_held = tied(mixed_heads, mlp_held)
    gate_up_near = gather_plane_near(mlp_held[:, : 2 * width_ff])
    down_held = mlp_held[:, 2 * width_ff :]
    saved = (query, key, value, pre, log_total)
    residual = residual_in + scatter_tokens(
        contract_cols(mixed_heads, out_full).astype(bf16), True
    )
    residual, down_held, out_grad = tied(residual, down_held, out_grad)
    out_grad = swap(out_grad)
    normed_mlp = rms_norm(residual, gain_mlp).astype(jnp.bfloat16)
    mlp_pair = gather_near(normed_mlp, False)
    mlp_pair, down_held, gate_up_near = tied(mlp_pair, down_held, gate_up_near)
    gate_up_full = gather_plane_far(gate_up_near)
    down_full = gather_plane(down_held)
    mlp_rows = gather_across(mlp_pair, False)
    cot_rows = gather_across(gather_near(out_grad, False), False)
    gate_up = matmul(mlp_rows, gate_up_full)
    gate_value = gate_up[:, :width_ff]
    up_value = gate_up[:, width_ff:]
    activated = (jax.nn.silu(gate_value) * up_value).astype(jnp.bfloat16)
    block_part = contract_cols(activated, down_full).astype(bf16)
    down_grad = contract_rows(cot_rows, activated).astype(bf16)
    cot_rows, down_grad = tied(cot_rows, down_grad)
    down_pieces = sum_plane(down_grad)
    d_activated = matmul(cot_rows, down_full)

    def swiglu(gate_in, up_in):
        return jax.nn.silu(gate_in) * up_in

    swiglu_out, swiglu_pull = jax.vjp(swiglu, gate_value, up_value)
    d_gate, d_up = swiglu_pull(d_activated)
    d_gate = d_gate.astype(jnp.bfloat16)
    d_up = d_up.astype(jnp.bfloat16)
    d_gate_up = jnp.concatenate([d_gate, d_up], axis=1)
    gate_up_grad = contract_rows(mlp_rows, d_gate_up)
    gate_up_pieces = sum_plane(gate_up_grad.astype(bf16))
    d_normed_mlp = scatter_tokens(contract_cols(d_gate_up, gate_up_full).astype(bf16), False)
    norm_out, norm_pull = jax.vjp(rms_norm, residual, gain_mlp)
    d_residual_norm, d_gain_mlp = norm_pull(d_normed_mlp)
    d_residual = out_grad.astype(jnp.float32) + d_residual_norm
    state_pair = gather_near(d_residual.astype(bf16), True)
    state_rows = gather_across(state_pair, True)
    out_chunks = sum_far(contract_rows(state_rows, mixed_heads).astype(bf16))
    d_heads, d_gain_heads = attention_backward(
        state_rows, out_full, saved, cosine_part, sine_part, gain_query, gain_key, start
    )
    d_heads, gate_up_pieces, down_pieces, block_part, out_chunks = tied(
        d_heads, gate_up_pieces, down_pieces, block_part, out_chunks
    )
    gate_up_held = cross_sum(gate_up_pieces)
    down_held = cross_sum(down_pieces)
    out_pieces = sum_near(out_chunks)
    heads_grad = contract_rows(attn_rows, d_heads)
    late_chunks = sum_far(heads_grad.astype(bf16))
    late_chunks, out_pieces = tied(late_chunks, out_pieces)
    late_pieces = sum_near(late_chunks)
    out_held = cross_sum(out_pieces)
    late_pieces, gate_up_held, down_held, out_held = tied(
        late_pieces, gate_up_held, down_held, out_held
    )
    late_held = cross_sum(late_pieces)
    gate_up_sum = finish_sum(gate_up_held)
    down_sum = finish_sum(down_held)
    d_normed_pair = scatter_across(contract_cols(d_heads, heads_full).astype(bf16), True)
    block_pair = scatter_across(block_part, False)
    late_held, d_normed_pair, block_pair = tied(late_held, d_normed_pair, block_pair)
    late_sum = finish_sum(late_held)
    out_sum = finish_sum(out_held)
    d_normed = scatter_near(d_normed_pair, True)
    block_out = (residual + scatter_near(block_pair, False)).astype(bf16)
    masters = (
        query_weight,
        key_matrix,
        value_matrix,
        out_weight,
        gate_weight,
        up_weight,
        down_weight,
    )
    moments = (
        query_moment,
        key_momentum,
        value_momentum,
        out_moment,
        gate_moment,
        up_moment,
        down_moment,
    )
    homes = {4: 0, 5: 3, 6: 4, 0: 7, 3: 5, 1: 1, 2: 2}
    group = tuple(range(7))
    reduced, fresh, slots = advance(
        (late_sum, out_sum, gate_up_sum, down_sum), moments, homes, lax.axis_size(DP)
    )
    owned = to_columns(slots)
    owned, d_normed = tied(owned, d_normed)
    pieces = to_homes(group, homes, owned)
    input_out, input_pull = jax.vjp(rms_norm, residual_in, gain_attn)
    d_input_norm, d_gain_attn = input_pull(d_normed)
    input_grad = (d_residual + d_input_norm).astype(bf16)
    gain_grad = jnp.concatenate([d_gain_attn, d_gain_mlp, d_gain_heads.reshape(-1)])
    gain_grad = sum_everywhere(gain_grad, [(name, lax.axis_size(name)) for name in ("core", "pl")])
    pieces, input_grad, block_out, gain_grad = tied(pieces, input_grad, block_out, gain_grad)
    back = orthogonalize(owns(group, homes), pieces)
    input_grad = swap(input_grad)
    block_out = swap(block_out)
    gain_grad = sum_everywhere(gain_grad, [("lo", lax.axis_size("lo"))])
    back, input_grad, block_out, gain_grad = tied(back, input_grad, block_out, gain_grad)
    input_grad = input_grad.astype(jnp.float32)
    block_out = block_out.astype(jnp.float32)
    gain_grad = sum_everywhere(gain_grad, [("hi", 2)])
    updated = update(from_columns(from_homes(group, homes, back)), masters, homes)
    first_next = BETA_FIRST * gain_first + (1.0 - BETA_FIRST) * gain_grad
    second_next = BETA_SECOND * gain_second + (1.0 - BETA_SECOND) * gain_grad * gain_grad
    first_hat = first_next / (1.0 - BETA_FIRST**ADAM_STEP)
    second_hat = second_next / (1.0 - BETA_SECOND**ADAM_STEP)
    gains_next = gains - GAIN_RATE * first_hat / (jnp.sqrt(second_hat) + ADAM_EPS)
    return (
        block_out,
        input_grad,
        reduced[0],
        reduced[1],
        reduced[2],
        reduced[3],
        reduced[4],
        reduced[5],
        reduced[6],
        updated[0],
        updated[1],
        updated[2],
        updated[3],
        updated[4],
        updated[5],
        updated[6],
        fresh[0],
        fresh[1],
        fresh[2],
        fresh[3],
        fresh[4],
        fresh[5],
        fresh[6],
        first_next,
        second_next,
        gains_next,
    )


def solution(mesh):
    dp_count, tensor_count = mesh.shape["dp"], mesh.shape["tensor"]
    split = Mesh(
        mesh.devices.reshape(dp_count // 2, 2, 2, tensor_count // 2), ("pl", "core", "hi", "lo")
    )
    tokens = P(("pl", "core", "hi", "lo"), None)
    rows = P(DP, TENSOR)
    columns = P(TENSOR, DP)
    matrices = (rows, rows, rows, columns, rows, rows, columns)
    whole = (P(), P(), P())
    return jax.shard_map(
        on_device,
        mesh=split,
        in_specs=(tokens, tokens, P(DP)) + matrices + matrices + whole,
        out_specs=(tokens, tokens) + matrices + matrices + matrices + whole,
        check_vma=False,
    )
```

```python
import functools
import math

import jax
import jax.numpy as jnp
from jax import lax
from jax.experimental import pallas as pl
from jax.experimental.pallas import tpu as pltpu
from jax.sharding import Mesh, PartitionSpec as P

MODEL_WIDTH = 1024
QUERY_HEADS = 16
KEY_VALUE_HEADS = 8
HEAD_SIZE = 128
FF = 3072
NS_STEPS = 5
ADAM_STEP = 10


EPS_NORM = 1e-06
ROPE_BASE = 1000000.0
MASK_FILL = -1e30
MOMENTUM = 0.95
COEF_LINEAR = 3.4445
COEF_GRAM = -4.775
COEF_SQUARE = 2.0315
NS_EPS = 1e-07
DECAY_KEEP = 0.998
BETA_FIRST = 0.9
BETA_SECOND = 0.95
ADAM_EPS = 1e-08
GAIN_RATE = 0.6
ROW_BLOCK = 256


DP = ("pl", "core")
TENSOR = ("hi", "lo")


def matmul(left, right):
    return jnp.dot(left, right, preferred_element_type=jnp.float32)


def contract_rows(left, right):
    return lax.dot_general(
        left, right, (((0,), (0,)), ((), ())), preferred_element_type=jnp.float32
    )


def contract_cols(left, right):
    return lax.dot_general(
        left, right, (((1,), (1,)), ((), ())), preferred_element_type=jnp.float32
    )


def orthogonalize_kernel(owner_ref, *refs):
    count = (len(refs) - 4) // 3

    @pl.when(owner_ref[0] != 0)
    def _():
        orthogonalize_owned(count, refs)

    @pl.when(owner_ref[0] == 0)
    def _():
        for result in refs[count : 3 * count]:
            result[...] = jnp.zeros_like(result)


def orthogonalize_owned(count, refs):
    pieces, results = refs[:count], refs[count : 3 * count]
    current, gram, gram_low, mixing = refs[3 * count :]
    size, width = pieces[0].shape
    block = 256
    blocks = size // block
    for number, piece in enumerate(pieces):
        current[:, number * width : (number + 1) * width] = piece[...]
    diagonal = lax.broadcasted_iota(jnp.int32, (block, block), 0) == lax.broadcasted_iota(
        jnp.int32, (block, block), 1
    )

    def mix(number):
        for col in range(blocks):
            at = col * block
            gram[at:, at : at + block] = contract_cols(current[at:, :], current[at : at + block, :])
        trace = jnp.float32(0.0)
        for col in range(blocks):
            at = col * block
            trace += jnp.sum(jnp.where(diagonal, gram[at : at + block, at : at + block], 0.0))
        scale = jnp.where(number == 0, 1.0 / (jnp.sqrt(trace) + NS_EPS), 1.0)
        scale_square = scale * scale
        for col in range(blocks):
            at = col * block
            for row in range(col, blocks):
                to = row * block
                tile = gram[to : to + block, at : at + block] * scale_square
                gram[to : to + block, at : at + block] = tile
                gram_low[to : to + block, at : at + block] = tile.astype(jnp.bfloat16)
                if row > col:
                    gram_low[at : at + block, to : to + block] = tile.T.astype(jnp.bfloat16)
        for col in range(blocks):
            at = col * block
            square = matmul(gram_low[at:, :], gram_low[:, at : at + block])
            for row in range(col, blocks):
                to = row * block
                tile = COEF_GRAM * gram[to : to + block, at : at + block]
                tile += COEF_SQUARE * square[to - at : to - at + block]
                if row == col:
                    tile += jnp.where(diagonal, COEF_LINEAR, 0.0)
                tile = tile * scale
                mixing[to : to + block, at : at + block] = tile.astype(jnp.bfloat16)
                if row > col:
                    mixing[at : at + block, to : to + block] = tile.T.astype(jnp.bfloat16)

    def sweep(number, carry):
        mix(number)

        def columns(step, inner):
            span = pl.ds(pl.multiple_of(step * width, width), width)
            current[:, span] = matmul(mixing[...], current[:, span]).astype(jnp.bfloat16)
            return inner

        lax.fori_loop(0, count, columns, 0)
        return carry

    lax.fori_loop(0, NS_STEPS, sweep, 0)
    for number, result in enumerate(results):
        at = number % count * width
        if number < count:
            result[...] = current[:, at : at + result.shape[1]]
        else:
            result[...] = current[:, at + width - result.shape[1] : at + width]


def orthogonalize(owner, pieces):
    size, width = pieces[0].shape
    first = (width // 2 + 127) // 128 * 128
    total = width * len(pieces)
    flops = NS_STEPS * 2 * size * size * (total * 13 // 8 + size * 5 // 8)
    return pl.pallas_call(
        orthogonalize_kernel,
        out_shape=[
            jax.ShapeDtypeStruct((size, part), piece.dtype)
            for part in (first, width - first)
            for piece in pieces
        ],
        in_specs=[pl.BlockSpec(memory_space=pltpu.SMEM)]
        + [pl.BlockSpec(memory_space=pltpu.VMEM)] * len(pieces),
        out_specs=[pl.BlockSpec(memory_space=pltpu.VMEM)] * (2 * len(pieces)),
        scratch_shapes=[
            pltpu.VMEM((size, total), jnp.bfloat16),
            pltpu.VMEM((size, size), jnp.float32),
            pltpu.VMEM((size, size), jnp.bfloat16),
            pltpu.VMEM((size, size), jnp.bfloat16),
        ],
        compiler_params=pltpu.CompilerParams(vmem_limit_bytes=48 * 1024 * 1024),
        cost_estimate=pl.CostEstimate(
            flops=flops, bytes_accessed=4 * size * total, transcendentals=0
        ),
    )(owner.astype(jnp.int32).reshape(1), *pieces)


def tied(*values):
    return lax.optimization_barrier(values)


def swap(values):
    return lax.ppermute(values, ("core", "hi"), [(0, 0), (1, 2), (2, 1), (3, 3)])


def to_partner(values, name):
    return lax.ppermute(values, name, [(0, 1), (1, 0)])


def in_order(first, mine, theirs):
    return jnp.concatenate([jnp.where(first, mine, theirs), jnp.where(first, theirs, mine)], axis=0)


def half_of(values, which):
    rows = values.shape[0] // 2
    return lax.dynamic_slice_in_dim(values, which * rows, rows, 0)


def gather_near(values, ordered):
    if lax.axis_size("lo") == 2:
        other = to_partner(values, "lo")
        if ordered:
            return in_order(lax.axis_index("lo") == 0, values, other)
        return jnp.concatenate([values, other], axis=0)
    return lax.all_gather(values, "lo", axis=0, tiled=True)


def gather_across(pair, ordered):
    other = to_partner(pair, "core")
    if ordered:
        return in_order(lax.axis_index("core") == 0, pair, other)
    return jnp.concatenate([pair, other], axis=0)


def scatter_across(values, ordered):
    place = lax.axis_index("core") if ordered else 0
    received = to_partner(half_of(values, 1 - place), "core").astype(jnp.float32)
    return half_of(values, place).astype(jnp.float32) + received


def scatter_near(pair, ordered):
    if lax.axis_size("lo") == 2:
        place = lax.axis_index("lo") if ordered else 0
        received = to_partner(half_of(pair, 1 - place).astype(jnp.bfloat16), "lo")
        return half_of(pair, place) + received.astype(jnp.float32)
    return lax.psum_scatter(
        pair.astype(jnp.bfloat16), "lo", scatter_dimension=0, tiled=True
    ).astype(jnp.float32)


def scatter_tokens(values, ordered):
    return scatter_near(scatter_across(values, ordered), ordered)


def both_cores(shard):
    return in_order(lax.axis_index("core") == 0, shard, to_partner(shard, "core"))


def exchange(values, stride):
    count = lax.axis_size("pl")
    return lax.ppermute(values, "pl", [(index, index ^ stride) for index in range(count)])


def in_places(found, held):
    rows = held.shape[0] * lax.axis_size("pl")
    full = jnp.zeros((rows, held.shape[1]), held.dtype)
    for piece, at in found:
        full = lax.dynamic_update_slice_in_dim(full, piece, at, 0)
    return full


def gather_plane_direct(held):
    place = lax.axis_index("pl")
    rows = held.shape[0]
    found = [(held, place * rows)]
    for stride in range(1, lax.axis_size("pl")):
        found.append((exchange(held, stride), (place ^ stride) * rows))
    return in_places(found, held)


def gather_plane_near(held):
    if lax.axis_size("pl") != 4:
        return [held] + [exchange(held, stride) for stride in range(1, lax.axis_size("pl"))]
    return [held, exchange(held, 1), exchange(held, 2)]


def gather_plane_far(near):
    place = lax.axis_index("pl")
    rows = near[0].shape[0]
    half = rows // 2
    found = [(piece, (place ^ stride) * rows) for stride, piece in enumerate(near)]
    if lax.axis_size("pl") == 4:
        found.append((exchange(near[2][:half], 1), (place ^ 3) * rows))
        found.append((exchange(near[1][half:], 2), (place ^ 3) * rows + half))
    return in_places(found, near[0])


def gather_plane(held):
    return gather_plane_far(gather_plane_near(held))


def sum_far(values):
    count = lax.axis_size("pl")
    place = lax.axis_index("pl")
    rows = values.shape[0] // count
    half = rows // 2
    chunks = [
        lax.dynamic_slice_in_dim(values, (place ^ stride) * rows, rows, 0) for stride in range(count)
    ]
    if count != 4:
        return chunks
    return chunks[:3] + [exchange(chunks[3][half:], 2), exchange(chunks[3][:half], 1)]


def sum_near(chunks):
    count = lax.axis_size("pl")
    if count != 4:
        return chunks[:1] + [exchange(chunks[stride], stride) for stride in range(1, count)]
    mine, first, second, for_first, for_second = chunks
    half = mine.shape[0] // 2
    first = jnp.concatenate([first[:half], add(first[half:], for_first)], axis=0)
    second = jnp.concatenate([add(second[:half], for_second), second[half:]], axis=0)
    return [mine, exchange(first, 1), exchange(second, 2)]


def sum_plane(values):
    return sum_near(sum_far(values))


def add(left, right):
    return (left.astype(jnp.float32) + right.astype(jnp.float32)).astype(jnp.bfloat16)


def cross_sum(pieces):
    total = sum(piece.astype(jnp.float32) for piece in pieces)
    return swap(total.astype(jnp.bfloat16))


def finish_sum(held):
    place = lax.axis_index("core")
    received = to_partner(half_of(held, 1 - place), "core")
    return half_of(held, place).astype(jnp.float32) + received.astype(jnp.float32)


def sum_everywhere(values, sizes):
    for name, count in sizes:
        stride = 1
        while stride < count:
            pairs = [(index, index ^ stride) for index in range(count)]
            values = values + lax.ppermute(values, name, pairs)
            stride *= 2
    return values


def rms_norm(values, gain):
    return values * lax.rsqrt(jnp.mean(values * values, axis=-1, keepdims=True) + EPS_NORM) * gain


def rotary(positions):
    half_width = HEAD_SIZE // 2
    inverse = jnp.power(
        jnp.float32(ROPE_BASE), -(jnp.arange(half_width, dtype=jnp.float32) * (2.0 / HEAD_SIZE))
    )
    angles = positions.astype(jnp.float32)[:, None] * inverse[None, :]
    cosine_part = jnp.cos(angles)
    sine_part = jnp.sin(angles)
    return (
        jnp.concatenate([cosine_part, cosine_part], axis=-1),
        jnp.concatenate([-sine_part, sine_part], axis=-1),
    )


def visible_pairs(start_ref, block, extent, rows):
    query = block * rows + lax.broadcasted_iota(jnp.int32, (extent, rows), 1)
    key = lax.broadcasted_iota(jnp.int32, (extent, rows), 0)
    begin = start_ref[:, block * rows : (block + 1) * rows]
    return (key <= query) & (key >= begin)


def turn_half(values):
    return pltpu.roll(values, HEAD_SIZE // 2, 1)


def project_kernel(
    rows_ref,
    weight_ref,
    cosine_ref,
    sine_ref,
    gain_query_ref,
    gain_key_ref,
    query_ref,
    key_ref,
    value_ref,
    pre_ref,
):
    total_rows = rows_ref.shape[0]
    width_query, width_key = query_ref.shape[1], key_ref.shape[1]
    size = ROW_BLOCK
    low = jnp.bfloat16

    def project(block, carry):
        span = pl.ds(pl.multiple_of(block * size, size), size)
        pre = matmul(rows_ref[span, :], weight_ref[...])
        pre_ref[span, :] = pre[:, : width_query + width_key]
        cosine, sine = cosine_ref[span, :], sine_ref[span, :]
        for at in range(0, width_query + width_key, HEAD_SIZE):
            gain_ref = gain_query_ref if at < width_query else gain_key_ref
            normal = rms_norm(pre[:, at : at + HEAD_SIZE], gain_ref[...])
            turned = (normal * cosine + turn_half(normal) * sine).astype(low)
            if at < width_query:
                query_ref[span, at : at + HEAD_SIZE] = turned
            else:
                key_ref[span, at - width_query : at - width_query + HEAD_SIZE] = turned
        value_ref[span, :] = pre[:, width_query + width_key :].astype(low)
        return carry

    lax.fori_loop(0, total_rows // size, project, 0)


def attend_kernel(
    query_ref, key_ref, value_ref, start_ref, mixed_ref, log_total_ref, turned_value
):
    total_rows = query_ref.shape[0]
    width_query, width_key = query_ref.shape[1], key_ref.shape[1]
    size = ROW_BLOCK
    scale = HEAD_SIZE**-0.5
    low = jnp.bfloat16

    def prepare(block, carry):
        span = pl.ds(pl.multiple_of(block * size, size), size)
        for at in range(0, width_key, HEAD_SIZE):
            value = value_ref[span, at : at + HEAD_SIZE].astype(jnp.float32)
            turned_value[at : at + HEAD_SIZE, span] = value.T.astype(low)
        return carry

    lax.fori_loop(0, total_rows // size, prepare, 0)
    group = width_query // width_key
    for block in range(total_rows // size):
        extent = (block + 1) * size
        rows = slice(block * size, extent)
        visible = visible_pairs(start_ref, block, extent, size)
        for head in range(width_query // HEAD_SIZE):
            key_at = head // group * HEAD_SIZE
            lanes = slice(head * HEAD_SIZE, (head + 1) * HEAD_SIZE)
            key_lanes = slice(key_at, key_at + HEAD_SIZE)
            scores = contract_cols(key_ref[:extent, key_lanes], query_ref[rows, lanes])
            scores = jnp.where(visible, scores, MASK_FILL)
            row_max = jnp.max(scores, axis=0, keepdims=True)
            weights = jnp.exp((scores - row_max) * scale)
            total = jnp.sum(weights, axis=0, keepdims=True)
            log_total_ref[head : head + 1, rows] = row_max * scale + jnp.log(total)
            weights = (weights * (1.0 / total)).astype(low)
            mixed = matmul(turned_value[key_lanes, :extent], weights)
            mixed_ref[rows, lanes] = mixed.T.astype(low)


def attention_backward_kernel(
    state_ref,
    out_ref,
    query_ref,
    key_ref,
    value_ref,
    pre_ref,
    log_total_ref,
    cosine_ref,
    sine_ref,
    gain_query_ref,
    gain_key_ref,
    start_ref,
    d_heads_ref,
    d_gain_ref,
    d_mixed,
    turned_key,
    d_query,
    d_key,
    d_value,
):
    total_rows = state_ref.shape[0]
    width_query, width_key = query_ref.shape[1], key_ref.shape[1]
    size = ROW_BLOCK
    scale = HEAD_SIZE**-0.5
    low = jnp.bfloat16

    def prepare(block, carry):
        span = pl.ds(pl.multiple_of(block * size, size), size)
        d_mixed[span, :] = matmul(state_ref[span, :], out_ref[...]).astype(low)
        for at in range(0, width_key, HEAD_SIZE):
            key = key_ref[span, at : at + HEAD_SIZE].astype(jnp.float32)
            turned_key[at : at + HEAD_SIZE, span] = key.T.astype(low)
        return carry

    lax.fori_loop(0, total_rows // size, prepare, 0)
    d_key[...] = jnp.zeros_like(d_key)
    d_value[...] = jnp.zeros_like(d_value)
    group = width_query // width_key
    for block in range(total_rows // size):
        extent = (block + 1) * size
        rows = slice(block * size, extent)
        visible = visible_pairs(start_ref, block, extent, size)
        for head in range(width_query // HEAD_SIZE):
            key_at = head // group * HEAD_SIZE
            lanes = slice(head * HEAD_SIZE, (head + 1) * HEAD_SIZE)
            key_lanes = slice(key_at, key_at + HEAD_SIZE)
            query = query_ref[rows, lanes]
            cotangent = d_mixed[rows, lanes]
            scores = contract_cols(key_ref[:extent, key_lanes], query) * scale
            probs = jnp.exp(scores - log_total_ref[head : head + 1, rows])
            probs = jnp.where(visible, probs, 0.0)
            d_probs = contract_cols(value_ref[:extent, key_lanes], cotangent)
            shift = jnp.sum(d_probs * probs, axis=0, keepdims=True)
            d_scores = (probs * (d_probs - shift)).astype(low)
            d_value[:extent, key_lanes] += matmul(probs.astype(low), cotangent)
            d_key[:extent, key_lanes] += matmul(d_scores, query)
            d_query[rows, lanes] = matmul(turned_key[key_lanes, :extent], d_scores).T * scale

    def finish(block, carry):
        span = pl.ds(pl.multiple_of(block * size, size), size)
        cosine, sine = cosine_ref[span, :], sine_ref[span, :]
        sums = []
        for at in range(0, width_query + width_key, HEAD_SIZE):
            if at < width_query:
                gain, cotangent = gain_query_ref[...], d_query[span, at : at + HEAD_SIZE]
            else:
                begin = at - width_query
                gain = gain_key_ref[...]
                cotangent = d_key[span, begin : begin + HEAD_SIZE] * scale
            cotangent = cotangent * cosine - turn_half(cotangent) * sine
            pre = pre_ref[span, at : at + HEAD_SIZE]
            inverse = lax.rsqrt(jnp.mean(pre * pre, axis=-1, keepdims=True) + EPS_NORM)
            normal = pre * inverse
            sums.append(jnp.sum(cotangent * normal, axis=0, keepdims=True))
            pulled = cotangent * gain
            inner = jnp.mean(normal * pulled, axis=-1, keepdims=True)
            d_pre = inverse * (pulled - normal * inner)
            d_heads_ref[span, at : at + HEAD_SIZE] = d_pre.astype(low)
        d_heads_ref[span, width_query + width_key :] = d_value[span, :].astype(low)
        heads_query = width_query // HEAD_SIZE
        return carry[0] + sum(sums[:heads_query]), carry[1] + sum(sums[heads_query:])

    zero = jnp.zeros((1, HEAD_SIZE), jnp.float32)
    for_query, for_key = lax.fori_loop(0, total_rows // size, finish, (zero, zero))
    d_gain_ref[0:1, :] = for_query
    d_gain_ref[1:2, :] = for_key


def in_vmem(kernel, operands, results, scratch, flops):
    moved = sum(math.prod(item.shape) * item.dtype.itemsize for item in operands + results)
    return pl.pallas_call(
        kernel,
        out_shape=results,
        in_specs=[pl.BlockSpec(memory_space=pltpu.VMEM)] * len(operands),
        out_specs=[pl.BlockSpec(memory_space=pltpu.VMEM)] * len(results),
        scratch_shapes=scratch,
        compiler_params=pltpu.CompilerParams(vmem_limit_bytes=48 * 1024 * 1024),
        cost_estimate=pl.CostEstimate(flops=flops, bytes_accessed=moved, transcendentals=0),
    )(*operands)


def project(rows, weight, cosine, sine, gain_query, gain_key, width_query):
    total_rows, columns = rows.shape
    width_key = (weight.shape[1] - width_query) // 2
    low = jnp.bfloat16
    shape = jax.ShapeDtypeStruct
    return in_vmem(
        project_kernel,
        [rows, weight, cosine, sine, gain_query, gain_key],
        [
            shape((total_rows, width_query), low),
            shape((total_rows, width_key), low),
            shape((total_rows, width_key), low),
            shape((total_rows, width_query + width_key), jnp.float32),
        ],
        [],
        2 * total_rows * columns * weight.shape[1],
    )


def attend(query, key, value, start):
    total_rows, width_query = query.shape
    width_key = key.shape[1]
    shape = jax.ShapeDtypeStruct
    return in_vmem(
        attend_kernel,
        [query, key, value, start],
        [
            shape((total_rows, width_query), jnp.bfloat16),
            shape((width_query // HEAD_SIZE, total_rows), jnp.float32),
        ],
        [pltpu.VMEM((width_key, total_rows), jnp.bfloat16)],
        4 * total_rows * total_rows * width_query,
    )


def attention_backward(
    state, out_full, saved, cosine, sine, gain_query, gain_key, start
):
    query, key, value, pre, log_total = saved
    total_rows, columns = state.shape
    width_query, width_key = query.shape[1], key.shape[1]
    low = jnp.bfloat16
    shape = jax.ShapeDtypeStruct
    return in_vmem(
        attention_backward_kernel,
        [state, out_full, query, key, value, pre, log_total]
        + [cosine, sine, gain_query, gain_key, start],
        [
            shape((total_rows, width_query + 2 * width_key), low),
            shape((2, HEAD_SIZE), jnp.float32),
        ],
        [
            pltpu.VMEM((total_rows, width_query), low),
            pltpu.VMEM((width_key, total_rows), low),
            pltpu.VMEM((total_rows, width_query), jnp.float32),
            pltpu.VMEM((total_rows, width_key), jnp.float32),
            pltpu.VMEM((total_rows, width_key), jnp.float32),
        ],
        2 * total_rows * columns * width_query + 10 * total_rows * total_rows * width_query,
    )


def home_row(index):
    return lax.axis_size(TENSOR) // 2 - 1 + index % 2


def owns(group, homes):
    index, row = lax.axis_index(DP), lax.axis_index(TENSOR)
    mine = functools.reduce(jnp.logical_or, [index == homes[number] for number in group])
    return mine & (row == home_row(index))


def toward_home(group, homes, step):
    rows = lax.axis_size(TENSOR)
    return [
        (index * rows + (home_row(index) + step) % rows, index * rows + home_row(index))
        for index in sorted(homes[number] for number in group)
    ]


def to_columns(slots):
    owned = lax.all_to_all(slots, DP, split_axis=0, concat_axis=0, tiled=True)
    return owned.reshape(-1, slots.shape[2])


def to_homes(group, homes, owned):
    return [owned] + [
        lax.ppermute(owned, DP + TENSOR, toward_home(group, homes, step))
        for step in range(1, lax.axis_size(TENSOR))
    ]


def from_homes(group, homes, back):
    index, row = lax.axis_index(DP), lax.axis_index(TENSOR)
    received = jnp.where(row == home_row(index), back[0], jnp.zeros_like(back[0]))
    for step in range(1, lax.axis_size(TENSOR)):
        pairs = [(target, source) for source, target in toward_home(group, homes, step)]
        received = received + lax.ppermute(back[step], DP + TENSOR, pairs)
    return received


def from_columns(received):
    shape = (lax.axis_size(DP), -1, received.shape[1])
    return lax.all_to_all(received.reshape(shape), DP, split_axis=0, concat_axis=0, tiled=True)


FLIPPED = (False, False, False, True, False, False, True)
SHAPES = (
    (MODEL_WIDTH, QUERY_HEADS * HEAD_SIZE),
    (MODEL_WIDTH, KEY_VALUE_HEADS * HEAD_SIZE),
    (MODEL_WIDTH, KEY_VALUE_HEADS * HEAD_SIZE),
    (QUERY_HEADS * HEAD_SIZE, MODEL_WIDTH),
    (MODEL_WIDTH, FF),
    (MODEL_WIDTH, FF),
    (FF, MODEL_WIDTH),
)
FANS = (
    MODEL_WIDTH,
    MODEL_WIDTH,
    MODEL_WIDTH,
    QUERY_HEADS * HEAD_SIZE // 64,
    MODEL_WIDTH,
    MODEL_WIDTH,
    FF,
)


def advance_kernel(homes, *refs):
    late_ref, out_ref, gate_up_ref, down_ref = refs[:4]
    moment_refs, reduced_refs, fresh_refs = refs[4:11], refs[11:18], refs[18:25]
    slots_ref = refs[25]
    width_query, width_key = moment_refs[0].shape[1], moment_refs[1].shape[1]
    width_ff = moment_refs[4].shape[1]
    gradients = (
        late_ref[:, :width_query],
        late_ref[:, width_query : width_query + width_key],
        late_ref[:, width_query + width_key :],
        out_ref[...],
        gate_up_ref[:, :width_ff],
        gate_up_ref[:, width_ff:],
        down_ref[...],
    )
    slots_ref[...] = jnp.zeros_like(slots_ref)
    for number, gradient in enumerate(gradients):
        moment = moment_refs[number][...]
        if FLIPPED[number]:
            gradient_turned = gradient.T
            moment_next = MOMENTUM * moment + gradient_turned
            reduced_refs[number][...] = gradient_turned
            look = (gradient_turned + MOMENTUM * moment_next).T
        else:
            moment_next = MOMENTUM * moment + gradient
            reduced_refs[number][...] = gradient
            look = gradient + MOMENTUM * moment_next
        fresh_refs[number][...] = moment_next
        slots_ref[homes[number], :, : look.shape[1]] = look.astype(jnp.bfloat16)


def advance(sums, moments, homes, dp_count):
    rows = sums[0].shape[0]
    width = max(moment.shape[1] for moment in moments)
    shapes = [jax.ShapeDtypeStruct(moment.shape, jnp.float32) for moment in moments]
    results = in_vmem(
        functools.partial(advance_kernel, homes),
        list(sums) + list(moments),
        shapes + shapes + [jax.ShapeDtypeStruct((dp_count, rows, width), jnp.bfloat16)],
        [],
        0,
    )
    return results[:7], results[7:14], results[14]


def update_kernel(homes, *refs):
    returned_refs, refs = refs[:2], refs[2:]
    first = returned_refs[0].shape[2]
    for number in range(7):
        master_ref, result_ref = refs[number], refs[7 + number]
        width = master_ref.shape[0] if FLIPPED[number] else master_ref.shape[1]
        portion = returned_refs[0][homes[number], :, : min(width, first)]
        if width > first:
            rest = returned_refs[1][homes[number], :, : width - first]
            portion = jnp.concatenate([portion, rest], axis=1)
        portion = portion.astype(jnp.float32)
        if FLIPPED[number]:
            portion = portion.T
        step_size = 0.5 * FANS[number] ** (-0.5) * math.sqrt(max(SHAPES[number]))
        result_ref[...] = DECAY_KEEP * master_ref[...] - step_size * portion


def update(returned, masters, homes):
    return in_vmem(
        functools.partial(update_kernel, homes),
        list(returned) + list(masters),
        [jax.ShapeDtypeStruct(master.shape, jnp.float32) for master in masters],
        [],
        0,
    )


def on_device(
    hidden_in,
    out_grad,
    positions,
    query_weight,
    key_matrix,
    value_matrix,
    out_weight,
    gate_weight,
    up_weight,
    down_weight,
    query_moment,
    key_momentum,
    value_momentum,
    out_moment,
    gate_moment,
    up_moment,
    down_moment,
    gains,
    gain_first,
    gain_second,
):
    bf16 = jnp.bfloat16
    heads_local = jnp.concatenate(
        [query_weight.astype(bf16), key_matrix.astype(bf16), value_matrix.astype(bf16)], axis=1
    )
    out_local = out_weight.astype(bf16).T
    mlp_local = jnp.concatenate(
        [gate_weight.astype(bf16), up_weight.astype(bf16), down_weight.astype(bf16).T], axis=1
    )
    width_query = query_weight.shape[1]
    width_key = key_matrix.shape[1]
    width_ff = gate_weight.shape[1]
    heads_held = swap(both_cores(heads_local))
    hidden_in, positions, heads_held = tied(hidden_in, positions, heads_held)
    positions = swap(positions)
    hidden_in = swap(hidden_in)
    heads_near = gather_plane_near(heads_held)
    out_pair = both_cores(out_local)
    mlp_pair = both_cores(mlp_local)
    hidden_in, out_pair, heads_near = tied(hidden_in, out_pair, heads_near)
    heads_full = gather_plane_far(heads_near)
    out_held = swap(out_pair)
    gain_attn = gains[:MODEL_WIDTH]
    gain_mlp = gains[MODEL_WIDTH : 2 * MODEL_WIDTH]
    gain_query = gains[2 * MODEL_WIDTH : 2 * MODEL_WIDTH + HEAD_SIZE][None, :]
    gain_key = gains[2 * MODEL_WIDTH + HEAD_SIZE :][None, :]
    start = (jnp.arange(positions.shape[0], dtype=jnp.int32) - positions)[None, :]
    cosine_part, sine_part = rotary(positions)
    residual_in = hidden_in.astype(jnp.float32)
    normalized = rms_norm(residual_in, gain_attn).astype(jnp.bfloat16)

    attn_pair = gather_near(normalized, True)
    attn_pair, mlp_pair = tied(attn_pair, mlp_pair)
    mlp_held = swap(mlp_pair)
    attn_rows = gather_across(attn_pair, True)
    query, key, value, pre = project(
        attn_rows, heads_full, cosine_part, sine_part, gain_query, gain_key, width_query
    )
    query, out_held = tied(query, out_held)
    out_full = gather_plane_direct(out_held)
    mixed_heads, log_total = attend(query, key, value, start)
    mixed_heads, mlp_held = tied(mixed_heads, mlp_held)
    gate_up_near = gather_plane_near(mlp_held[:, : 2 * width_ff])
    down_held = mlp_held[:, 2 * width_ff :]
    saved = (query, key, value, pre, log_total)
    residual = residual_in + scatter_tokens(
        contract_cols(mixed_heads, out_full).astype(bf16), True
    )
    residual, down_held, out_grad = tied(residual, down_held, out_grad)
    out_grad = swap(out_grad)
    normed_mlp = rms_norm(residual, gain_mlp).astype(jnp.bfloat16)
    mlp_pair = gather_near(normed_mlp, False)
    mlp_pair, down_held, gate_up_near = tied(mlp_pair, down_held, gate_up_near)
    gate_up_full = gather_plane_far(gate_up_near)
    down_full = gather_plane(down_held)
    mlp_rows = gather_across(mlp_pair, False)
    cot_rows = gather_across(gather_near(out_grad, False), False)
    gate_up = matmul(mlp_rows, gate_up_full)
    gate_value = gate_up[:, :width_ff]
    up_value = gate_up[:, width_ff:]
    activated = (jax.nn.silu(gate_value) * up_value).astype(jnp.bfloat16)
    down_grad = contract_rows(cot_rows, activated).astype(bf16)
    cot_rows, down_grad = tied(cot_rows, down_grad)
    down_pieces = sum_plane(down_grad)
    d_activated = matmul(cot_rows, down_full)

    def swiglu(gate_in, up_in):
        return jax.nn.silu(gate_in) * up_in

    swiglu_out, swiglu_pull = jax.vjp(swiglu, gate_value, up_value)
    d_gate, d_up = swiglu_pull(d_activated)
    d_gate = d_gate.astype(jnp.bfloat16)
    d_up = d_up.astype(jnp.bfloat16)
    d_gate_up = jnp.concatenate([d_gate, d_up], axis=1)
    gate_up_grad = contract_rows(mlp_rows, d_gate_up)
    gate_up_pieces = sum_plane(gate_up_grad.astype(bf16))
    d_normed_mlp = scatter_tokens(contract_cols(d_gate_up, gate_up_full).astype(bf16), False)
    norm_out, norm_pull = jax.vjp(rms_norm, residual, gain_mlp)
    d_residual_norm, d_gain_mlp = norm_pull(d_normed_mlp)
    d_residual = out_grad.astype(jnp.float32) + d_residual_norm
    state_pair = gather_near(d_residual.astype(bf16), True)
    state_pair, down_pieces = tied(state_pair, down_pieces)
    state_rows = gather_across(state_pair, True)
    down_held = cross_sum(down_pieces)
    out_chunks = sum_far(contract_rows(state_rows, mixed_heads).astype(bf16))
    d_heads, d_gain_heads = attention_backward(
        state_rows, out_full, saved, cosine_part, sine_part, gain_query, gain_key, start
    )
    d_heads, gate_up_pieces, down_held, activated, out_chunks = tied(
        d_heads, gate_up_pieces, down_held, activated, out_chunks
    )
    block_part = contract_cols(activated, down_full).astype(bf16)
    gate_up_held = cross_sum(gate_up_pieces)
    out_pieces = sum_near(out_chunks)
    heads_grad = contract_rows(attn_rows, d_heads)
    late_chunks = sum_far(heads_grad.astype(bf16))
    late_chunks, out_pieces, d_heads = tied(late_chunks, out_pieces, d_heads)
    late_pieces = sum_near(late_chunks)
    out_held = cross_sum(out_pieces)
    late_pieces, gate_up_held, down_held, out_held = tied(
        late_pieces, gate_up_held, down_held, out_held
    )
    late_held = cross_sum(late_pieces)
    gate_up_sum = finish_sum(gate_up_held)
    down_sum = finish_sum(down_held)
    d_normed_pair = scatter_across(contract_cols(d_heads, heads_full).astype(bf16), True)
    block_pair = scatter_across(block_part, False)
    late_held, d_normed_pair, block_pair = tied(late_held, d_normed_pair, block_pair)
    late_sum = finish_sum(late_held)
    out_sum = finish_sum(out_held)
    d_normed = scatter_near(d_normed_pair, True)
    block_out = (residual + scatter_near(block_pair, False)).astype(bf16)
    masters = (
        query_weight,
        key_matrix,
        value_matrix,
        out_weight,
        gate_weight,
        up_weight,
        down_weight,
    )
    moments = (
        query_moment,
        key_momentum,
        value_momentum,
        out_moment,
        gate_moment,
        up_moment,
        down_moment,
    )
    homes = {4: 0, 5: 3, 6: 4, 0: 7, 3: 5, 1: 1, 2: 2}
    group = tuple(range(7))
    reduced, fresh, slots = advance(
        (late_sum, out_sum, gate_up_sum, down_sum), moments, homes, lax.axis_size(DP)
    )
    owned = to_columns(slots)
    owned, d_normed = tied(owned, d_normed)
    pieces = to_homes(group, homes, owned)
    input_out, input_pull = jax.vjp(rms_norm, residual_in, gain_attn)
    d_input_norm, d_gain_attn = input_pull(d_normed)
    input_grad = (d_residual + d_input_norm).astype(bf16)
    gain_grad = jnp.concatenate([d_gain_attn, d_gain_mlp, d_gain_heads.reshape(-1)])
    gain_grad = sum_everywhere(gain_grad, [(name, lax.axis_size(name)) for name in ("core", "pl")])
    pieces, input_grad, block_out, gain_grad = tied(pieces, input_grad, block_out, gain_grad)
    back = orthogonalize(owns(group, homes), pieces)
    gain_grad = sum_everywhere(gain_grad, [("lo", lax.axis_size("lo"))])
    back, input_grad, block_out, gain_grad = tied(back, input_grad, block_out, gain_grad)
    half = len(back) // 2
    received = [from_homes(group, homes, part) for part in (back[:half], back[half:])]
    input_grad = swap(input_grad).astype(jnp.float32)
    block_out = swap(block_out).astype(jnp.float32)
    received[1], gain_grad = tied(received[1], gain_grad)
    gain_grad = sum_everywhere(gain_grad, [("hi", 2)])
    updated = update([from_columns(part) for part in received], masters, homes)
    first_next = BETA_FIRST * gain_first + (1.0 - BETA_FIRST) * gain_grad
    second_next = BETA_SECOND * gain_second + (1.0 - BETA_SECOND) * gain_grad * gain_grad
    first_hat = first_next / (1.0 - BETA_FIRST**ADAM_STEP)
    second_hat = second_next / (1.0 - BETA_SECOND**ADAM_STEP)
    gains_next = gains - GAIN_RATE * first_hat / (jnp.sqrt(second_hat) + ADAM_EPS)
    return (
        block_out,
        input_grad,
        reduced[0],
        reduced[1],
        reduced[2],
        reduced[3],
        reduced[4],
        reduced[5],
        reduced[6],
        updated[0],
        updated[1],
        updated[2],
        updated[3],
        updated[4],
        updated[5],
        updated[6],
        fresh[0],
        fresh[1],
        fresh[2],
        fresh[3],
        fresh[4],
        fresh[5],
        fresh[6],
        first_next,
        second_next,
        gains_next,
    )


def solution(mesh):
    dp_count, tensor_count = mesh.shape["dp"], mesh.shape["tensor"]
    split = Mesh(
        mesh.devices.reshape(dp_count // 2, 2, 2, tensor_count // 2), ("pl", "core", "hi", "lo")
    )
    tokens = P(("pl", "core", "hi", "lo"), None)
    rows = P(DP, TENSOR)
    columns = P(TENSOR, DP)
    matrices = (rows, rows, rows, columns, rows, rows, columns)
    whole = (P(), P(), P())
    return jax.shard_map(
        on_device,
        mesh=split,
        in_specs=(tokens, tokens, P(DP)) + matrices + matrices + whole,
        out_specs=(tokens, tokens) + matrices + matrices + matrices + whole,
        check_vma=False,
    )
```

```python
import functools
import math

import jax
import jax.numpy as jnp
from jax import lax
from jax.experimental import pallas as pl
from jax.experimental.pallas import tpu as pltpu
from jax.sharding import Mesh, PartitionSpec as P

MODEL_WIDTH = 1024
QUERY_HEADS = 16
KEY_VALUE_HEADS = 8
HEAD_SIZE = 128
FF = 3072
NS_STEPS = 5
ADAM_STEP = 10


EPS_NORM = 1e-06
ROPE_BASE = 1000000.0
MASK_FILL = -1e30
MOMENTUM = 0.95
COEF_LINEAR = 3.4445
COEF_GRAM = -4.775
COEF_SQUARE = 2.0315
NS_EPS = 1e-07
DECAY_KEEP = 0.998
BETA_FIRST = 0.9
BETA_SECOND = 0.95
ADAM_EPS = 1e-08
GAIN_RATE = 0.6
ROW_BLOCK = 256


DP = ("pl", "core")
TENSOR = ("hi", "lo")


def matmul(left, right):
    return jnp.dot(left, right, preferred_element_type=jnp.float32)


def contract_rows(left, right):
    return lax.dot_general(
        left, right, (((0,), (0,)), ((), ())), preferred_element_type=jnp.float32
    )


def contract_cols(left, right):
    return lax.dot_general(
        left, right, (((1,), (1,)), ((), ())), preferred_element_type=jnp.float32
    )


def orthogonalize_kernel(owner_ref, *refs):
    count = (len(refs) - 4) // 3

    @pl.when(owner_ref[0] != 0)
    def _():
        orthogonalize_owned(count, refs)

    @pl.when(owner_ref[0] == 0)
    def _():
        for result in refs[count : 3 * count]:
            result[...] = jnp.zeros_like(result)


def orthogonalize_owned(count, refs):
    pieces, results = refs[:count], refs[count : 3 * count]
    current, gram, gram_low, mixing = refs[3 * count :]
    size, width = pieces[0].shape
    block = 256
    blocks = size // block
    for number, piece in enumerate(pieces):
        current[:, number * width : (number + 1) * width] = piece[...]
    diagonal = lax.broadcasted_iota(jnp.int32, (block, block), 0) == lax.broadcasted_iota(
        jnp.int32, (block, block), 1
    )

    def mix(number):
        for col in range(blocks):
            at = col * block
            gram[at:, at : at + block] = contract_cols(current[at:, :], current[at : at + block, :])
        trace = jnp.float32(0.0)
        for col in range(blocks):
            at = col * block
            trace += jnp.sum(jnp.where(diagonal, gram[at : at + block, at : at + block], 0.0))
        scale = jnp.where(number == 0, 1.0 / (jnp.sqrt(trace) + NS_EPS), 1.0)
        scale_square = scale * scale
        for col in range(blocks):
            at = col * block
            for row in range(col, blocks):
                to = row * block
                tile = gram[to : to + block, at : at + block] * scale_square
                gram[to : to + block, at : at + block] = tile
                gram_low[to : to + block, at : at + block] = tile.astype(jnp.bfloat16)
                if row > col:
                    gram_low[at : at + block, to : to + block] = tile.T.astype(jnp.bfloat16)
        for col in range(blocks):
            at = col * block
            square = matmul(gram_low[at:, :], gram_low[:, at : at + block])
            for row in range(col, blocks):
                to = row * block
                tile = COEF_GRAM * gram[to : to + block, at : at + block]
                tile += COEF_SQUARE * square[to - at : to - at + block]
                if row == col:
                    tile += jnp.where(diagonal, COEF_LINEAR, 0.0)
                tile = tile * scale
                mixing[to : to + block, at : at + block] = tile.astype(jnp.bfloat16)
                if row > col:
                    mixing[at : at + block, to : to + block] = tile.T.astype(jnp.bfloat16)

    def sweep(number, carry):
        mix(number)

        def columns(step, inner):
            span = pl.ds(pl.multiple_of(step * width, width), width)
            current[:, span] = matmul(mixing[...], current[:, span]).astype(jnp.bfloat16)
            return inner

        lax.fori_loop(0, count, columns, 0)
        return carry

    lax.fori_loop(0, NS_STEPS, sweep, 0)
    for number, result in enumerate(results):
        at = number % count * width
        if number < count:
            result[...] = current[:, at : at + result.shape[1]]
        else:
            result[...] = current[:, at + width - result.shape[1] : at + width]


def orthogonalize(owner, pieces):
    size, width = pieces[0].shape
    first = (width // 2 + 127) // 128 * 128
    total = width * len(pieces)
    flops = NS_STEPS * 2 * size * size * (total * 13 // 8 + size * 5 // 8)
    return pl.pallas_call(
        orthogonalize_kernel,
        out_shape=[
            jax.ShapeDtypeStruct((size, part), piece.dtype)
            for part in (first, width - first)
            for piece in pieces
        ],
        in_specs=[pl.BlockSpec(memory_space=pltpu.SMEM)]
        + [pl.BlockSpec(memory_space=pltpu.VMEM)] * len(pieces),
        out_specs=[pl.BlockSpec(memory_space=pltpu.VMEM)] * (2 * len(pieces)),
        scratch_shapes=[
            pltpu.VMEM((size, total), jnp.bfloat16),
            pltpu.VMEM((size, size), jnp.float32),
            pltpu.VMEM((size, size), jnp.bfloat16),
            pltpu.VMEM((size, size), jnp.bfloat16),
        ],
        compiler_params=pltpu.CompilerParams(vmem_limit_bytes=48 * 1024 * 1024),
        cost_estimate=pl.CostEstimate(
            flops=flops, bytes_accessed=4 * size * total, transcendentals=0
        ),
    )(owner.astype(jnp.int32).reshape(1), *pieces)


def tied(*values):
    return lax.optimization_barrier(values)


def swap(values):
    return lax.ppermute(values, ("core", "hi"), [(0, 0), (1, 2), (2, 1), (3, 3)])


def to_partner(values, name):
    return lax.ppermute(values, name, [(0, 1), (1, 0)])


def in_order(first, mine, theirs):
    return jnp.concatenate([jnp.where(first, mine, theirs), jnp.where(first, theirs, mine)], axis=0)


def half_of(values, which):
    rows = values.shape[0] // 2
    return lax.dynamic_slice_in_dim(values, which * rows, rows, 0)


def gather_near(values, ordered):
    if lax.axis_size("lo") == 2:
        other = to_partner(values, "lo")
        if ordered:
            return in_order(lax.axis_index("lo") == 0, values, other)
        return jnp.concatenate([values, other], axis=0)
    return lax.all_gather(values, "lo", axis=0, tiled=True)


def gather_across(pair, ordered):
    other = to_partner(pair, "core")
    if ordered:
        return in_order(lax.axis_index("core") == 0, pair, other)
    return jnp.concatenate([pair, other], axis=0)


def scatter_across(values, ordered):
    place = lax.axis_index("core") if ordered else 0
    received = to_partner(half_of(values, 1 - place), "core").astype(jnp.float32)
    return half_of(values, place).astype(jnp.float32) + received


def scatter_near(pair, ordered):
    if lax.axis_size("lo") == 2:
        place = lax.axis_index("lo") if ordered else 0
        received = to_partner(half_of(pair, 1 - place).astype(jnp.bfloat16), "lo")
        return half_of(pair, place) + received.astype(jnp.float32)
    return lax.psum_scatter(
        pair.astype(jnp.bfloat16), "lo", scatter_dimension=0, tiled=True
    ).astype(jnp.float32)


def scatter_tokens(values, ordered):
    return scatter_near(scatter_across(values, ordered), ordered)


def both_cores(shard):
    return in_order(lax.axis_index("core") == 0, shard, to_partner(shard, "core"))


def exchange(values, stride):
    count = lax.axis_size("pl")
    return lax.ppermute(values, "pl", [(index, index ^ stride) for index in range(count)])


def in_places(found, held):
    rows = held.shape[0] * lax.axis_size("pl")
    full = jnp.zeros((rows, held.shape[1]), held.dtype)
    for piece, at in found:
        full = lax.dynamic_update_slice_in_dim(full, piece, at, 0)
    return full


def gather_plane_direct(held):
    place = lax.axis_index("pl")
    rows = held.shape[0]
    found = [(held, place * rows)]
    for stride in range(1, lax.axis_size("pl")):
        found.append((exchange(held, stride), (place ^ stride) * rows))
    return in_places(found, held)


def gather_plane_near(held):
    if lax.axis_size("pl") != 4:
        return [held] + [exchange(held, stride) for stride in range(1, lax.axis_size("pl"))]
    return [held, exchange(held, 1), exchange(held, 2)]


def gather_plane_far(near):
    place = lax.axis_index("pl")
    rows = near[0].shape[0]
    half = rows // 2
    found = [(piece, (place ^ stride) * rows) for stride, piece in enumerate(near)]
    if lax.axis_size("pl") == 4:
        found.append((exchange(near[2][:half], 1), (place ^ 3) * rows))
        found.append((exchange(near[1][half:], 2), (place ^ 3) * rows + half))
    return in_places(found, near[0])


def gather_plane(held):
    return gather_plane_far(gather_plane_near(held))


def sum_far(values):
    count = lax.axis_size("pl")
    place = lax.axis_index("pl")
    rows = values.shape[0] // count
    half = rows // 2
    chunks = [
        lax.dynamic_slice_in_dim(values, (place ^ stride) * rows, rows, 0) for stride in range(count)
    ]
    if count != 4:
        return chunks
    return chunks[:3] + [exchange(chunks[3][half:], 2), exchange(chunks[3][:half], 1)]


def sum_near(chunks):
    count = lax.axis_size("pl")
    if count != 4:
        return chunks[:1] + [exchange(chunks[stride], stride) for stride in range(1, count)]
    mine, first, second, for_first, for_second = chunks
    half = mine.shape[0] // 2
    first = jnp.concatenate([first[:half], add(first[half:], for_first)], axis=0)
    second = jnp.concatenate([add(second[:half], for_second), second[half:]], axis=0)
    return [mine, exchange(first, 1), exchange(second, 2)]


def sum_plane(values):
    return sum_near(sum_far(values))


def add(left, right):
    return (left.astype(jnp.float32) + right.astype(jnp.float32)).astype(jnp.bfloat16)


def cross_sum(pieces):
    total = sum(piece.astype(jnp.float32) for piece in pieces)
    return swap(total.astype(jnp.bfloat16))


def finish_sum(held):
    place = lax.axis_index("core")
    received = to_partner(half_of(held, 1 - place), "core")
    return half_of(held, place).astype(jnp.float32) + received.astype(jnp.float32)


def sum_everywhere(values, sizes):
    for name, count in sizes:
        stride = 1
        while stride < count:
            pairs = [(index, index ^ stride) for index in range(count)]
            values = values + lax.ppermute(values, name, pairs)
            stride *= 2
    return values


def rms_norm(values, gain):
    return values * lax.rsqrt(jnp.mean(values * values, axis=-1, keepdims=True) + EPS_NORM) * gain


def rotary(positions):
    half_width = HEAD_SIZE // 2
    inverse = jnp.power(
        jnp.float32(ROPE_BASE), -(jnp.arange(half_width, dtype=jnp.float32) * (2.0 / HEAD_SIZE))
    )
    angles = positions.astype(jnp.float32)[:, None] * inverse[None, :]
    cosine_part = jnp.cos(angles)
    sine_part = jnp.sin(angles)
    return (
        jnp.concatenate([cosine_part, cosine_part], axis=-1),
        jnp.concatenate([-sine_part, sine_part], axis=-1),
    )


def visible_pairs(start_ref, block, extent, rows):
    query = block * rows + lax.broadcasted_iota(jnp.int32, (extent, rows), 1)
    key = lax.broadcasted_iota(jnp.int32, (extent, rows), 0)
    begin = start_ref[:, block * rows : (block + 1) * rows]
    return (key <= query) & (key >= begin)


def turn_half(values):
    return pltpu.roll(values, HEAD_SIZE // 2, 1)


def project_kernel(
    rows_ref,
    weight_ref,
    cosine_ref,
    sine_ref,
    gain_query_ref,
    gain_key_ref,
    query_ref,
    key_ref,
    value_ref,
    pre_ref,
):
    total_rows = rows_ref.shape[0]
    width_query, width_key = query_ref.shape[1], key_ref.shape[1]
    size = ROW_BLOCK
    low = jnp.bfloat16

    def project(block, carry):
        span = pl.ds(pl.multiple_of(block * size, size), size)
        pre = matmul(rows_ref[span, :], weight_ref[...])
        pre_ref[span, :] = pre[:, : width_query + width_key]
        cosine, sine = cosine_ref[span, :], sine_ref[span, :]
        for at in range(0, width_query + width_key, HEAD_SIZE):
            gain_ref = gain_query_ref if at < width_query else gain_key_ref
            normal = rms_norm(pre[:, at : at + HEAD_SIZE], gain_ref[...])
            turned = (normal * cosine + turn_half(normal) * sine).astype(low)
            if at < width_query:
                query_ref[span, at : at + HEAD_SIZE] = turned
            else:
                key_ref[span, at - width_query : at - width_query + HEAD_SIZE] = turned
        value_ref[span, :] = pre[:, width_query + width_key :].astype(low)
        return carry

    lax.fori_loop(0, total_rows // size, project, 0)


def attend_kernel(
    query_ref, key_ref, value_ref, start_ref, mixed_ref, log_total_ref, turned_value
):
    total_rows = query_ref.shape[0]
    width_query, width_key = query_ref.shape[1], key_ref.shape[1]
    size = ROW_BLOCK
    scale = HEAD_SIZE**-0.5
    low = jnp.bfloat16

    def prepare(block, carry):
        span = pl.ds(pl.multiple_of(block * size, size), size)
        for at in range(0, width_key, HEAD_SIZE):
            value = value_ref[span, at : at + HEAD_SIZE].astype(jnp.float32)
            turned_value[at : at + HEAD_SIZE, span] = value.T.astype(low)
        return carry

    lax.fori_loop(0, total_rows // size, prepare, 0)
    group = width_query // width_key
    for block in range(total_rows // size):
        extent = (block + 1) * size
        rows = slice(block * size, extent)
        visible = visible_pairs(start_ref, block, extent, size)
        for head in range(width_query // HEAD_SIZE):
            key_at = head // group * HEAD_SIZE
            lanes = slice(head * HEAD_SIZE, (head + 1) * HEAD_SIZE)
            key_lanes = slice(key_at, key_at + HEAD_SIZE)
            scores = contract_cols(key_ref[:extent, key_lanes], query_ref[rows, lanes])
            scores = jnp.where(visible, scores, MASK_FILL)
            row_max = jnp.max(scores, axis=0, keepdims=True)
            weights = jnp.exp((scores - row_max) * scale)
            total = jnp.sum(weights, axis=0, keepdims=True)
            log_total_ref[head : head + 1, rows] = row_max * scale + jnp.log(total)
            weights = (weights * (1.0 / total)).astype(low)
            mixed = matmul(turned_value[key_lanes, :extent], weights)
            mixed_ref[rows, lanes] = mixed.T.astype(low)


def attention_backward_kernel(
    state_ref,
    out_ref,
    query_ref,
    key_ref,
    value_ref,
    pre_ref,
    log_total_ref,
    cosine_ref,
    sine_ref,
    gain_query_ref,
    gain_key_ref,
    start_ref,
    d_heads_ref,
    d_gain_ref,
    d_mixed,
    turned_key,
    d_query,
    d_key,
    d_value,
):
    total_rows = state_ref.shape[0]
    width_query, width_key = query_ref.shape[1], key_ref.shape[1]
    size = ROW_BLOCK
    scale = HEAD_SIZE**-0.5
    low = jnp.bfloat16

    def prepare(block, carry):
        span = pl.ds(pl.multiple_of(block * size, size), size)
        d_mixed[span, :] = matmul(state_ref[span, :], out_ref[...]).astype(low)
        for at in range(0, width_key, HEAD_SIZE):
            key = key_ref[span, at : at + HEAD_SIZE].astype(jnp.float32)
            turned_key[at : at + HEAD_SIZE, span] = key.T.astype(low)
        return carry

    lax.fori_loop(0, total_rows // size, prepare, 0)
    d_key[...] = jnp.zeros_like(d_key)
    d_value[...] = jnp.zeros_like(d_value)
    group = width_query // width_key
    for block in range(total_rows // size):
        extent = (block + 1) * size
        rows = slice(block * size, extent)
        visible = visible_pairs(start_ref, block, extent, size)
        for head in range(width_query // HEAD_SIZE):
            key_at = head // group * HEAD_SIZE
            lanes = slice(head * HEAD_SIZE, (head + 1) * HEAD_SIZE)
            key_lanes = slice(key_at, key_at + HEAD_SIZE)
            query = query_ref[rows, lanes]
            cotangent = d_mixed[rows, lanes]
            scores = contract_cols(key_ref[:extent, key_lanes], query) * scale
            probs = jnp.exp(scores - log_total_ref[head : head + 1, rows])
            probs = jnp.where(visible, probs, 0.0)
            d_probs = contract_cols(value_ref[:extent, key_lanes], cotangent)
            shift = jnp.sum(d_probs * probs, axis=0, keepdims=True)
            d_scores = (probs * (d_probs - shift)).astype(low)
            d_value[:extent, key_lanes] += matmul(probs.astype(low), cotangent)
            d_key[:extent, key_lanes] += matmul(d_scores, query)
            d_query[rows, lanes] = matmul(turned_key[key_lanes, :extent], d_scores).T * scale

    def finish(block, carry):
        span = pl.ds(pl.multiple_of(block * size, size), size)
        cosine, sine = cosine_ref[span, :], sine_ref[span, :]
        sums = []
        for at in range(0, width_query + width_key, HEAD_SIZE):
            if at < width_query:
                gain, cotangent = gain_query_ref[...], d_query[span, at : at + HEAD_SIZE]
            else:
                begin = at - width_query
                gain = gain_key_ref[...]
                cotangent = d_key[span, begin : begin + HEAD_SIZE] * scale
            cotangent = cotangent * cosine - turn_half(cotangent) * sine
            pre = pre_ref[span, at : at + HEAD_SIZE]
            inverse = lax.rsqrt(jnp.mean(pre * pre, axis=-1, keepdims=True) + EPS_NORM)
            normal = pre * inverse
            sums.append(jnp.sum(cotangent * normal, axis=0, keepdims=True))
            pulled = cotangent * gain
            inner = jnp.mean(normal * pulled, axis=-1, keepdims=True)
            d_pre = inverse * (pulled - normal * inner)
            d_heads_ref[span, at : at + HEAD_SIZE] = d_pre.astype(low)
        d_heads_ref[span, width_query + width_key :] = d_value[span, :].astype(low)
        heads_query = width_query // HEAD_SIZE
        return carry[0] + sum(sums[:heads_query]), carry[1] + sum(sums[heads_query:])

    zero = jnp.zeros((1, HEAD_SIZE), jnp.float32)
    for_query, for_key = lax.fori_loop(0, total_rows // size, finish, (zero, zero))
    d_gain_ref[0:1, :] = for_query
    d_gain_ref[1:2, :] = for_key


def in_vmem(kernel, operands, results, scratch, flops):
    moved = sum(math.prod(item.shape) * item.dtype.itemsize for item in operands + results)
    return pl.pallas_call(
        kernel,
        out_shape=results,
        in_specs=[pl.BlockSpec(memory_space=pltpu.VMEM)] * len(operands),
        out_specs=[pl.BlockSpec(memory_space=pltpu.VMEM)] * len(results),
        scratch_shapes=scratch,
        compiler_params=pltpu.CompilerParams(vmem_limit_bytes=48 * 1024 * 1024),
        cost_estimate=pl.CostEstimate(flops=flops, bytes_accessed=moved, transcendentals=0),
    )(*operands)


def project(rows, weight, cosine, sine, gain_query, gain_key, width_query):
    total_rows, columns = rows.shape
    width_key = (weight.shape[1] - width_query) // 2
    low = jnp.bfloat16
    shape = jax.ShapeDtypeStruct
    return in_vmem(
        project_kernel,
        [rows, weight, cosine, sine, gain_query, gain_key],
        [
            shape((total_rows, width_query), low),
            shape((total_rows, width_key), low),
            shape((total_rows, width_key), low),
            shape((total_rows, width_query + width_key), jnp.float32),
        ],
        [],
        2 * total_rows * columns * weight.shape[1],
    )


def attend(query, key, value, start):
    total_rows, width_query = query.shape
    width_key = key.shape[1]
    shape = jax.ShapeDtypeStruct
    return in_vmem(
        attend_kernel,
        [query, key, value, start],
        [
            shape((total_rows, width_query), jnp.bfloat16),
            shape((width_query // HEAD_SIZE, total_rows), jnp.float32),
        ],
        [pltpu.VMEM((width_key, total_rows), jnp.bfloat16)],
        4 * total_rows * total_rows * width_query,
    )


def attention_backward(
    state, out_full, saved, cosine, sine, gain_query, gain_key, start
):
    query, key, value, pre, log_total = saved
    total_rows, columns = state.shape
    width_query, width_key = query.shape[1], key.shape[1]
    low = jnp.bfloat16
    shape = jax.ShapeDtypeStruct
    return in_vmem(
        attention_backward_kernel,
        [state, out_full, query, key, value, pre, log_total]
        + [cosine, sine, gain_query, gain_key, start],
        [
            shape((total_rows, width_query + 2 * width_key), low),
            shape((2, HEAD_SIZE), jnp.float32),
        ],
        [
            pltpu.VMEM((total_rows, width_query), low),
            pltpu.VMEM((width_key, total_rows), low),
            pltpu.VMEM((total_rows, width_query), jnp.float32),
            pltpu.VMEM((total_rows, width_key), jnp.float32),
            pltpu.VMEM((total_rows, width_key), jnp.float32),
        ],
        2 * total_rows * columns * width_query + 10 * total_rows * total_rows * width_query,
    )


def home_row(index):
    return lax.axis_size(TENSOR) // 2 - 1 + index % 2


def owns(group, homes):
    index, row = lax.axis_index(DP), lax.axis_index(TENSOR)
    mine = functools.reduce(jnp.logical_or, [index == homes[number] for number in group])
    return mine & (row == home_row(index))


def toward_home(group, homes, step):
    rows = lax.axis_size(TENSOR)
    return [
        (index * rows + (home_row(index) + step) % rows, index * rows + home_row(index))
        for index in sorted(homes[number] for number in group)
    ]


def to_columns(slots):
    owned = lax.all_to_all(slots, DP, split_axis=0, concat_axis=0, tiled=True)
    return owned.reshape(-1, slots.shape[2])


def to_homes(group, homes, owned):
    return [owned] + [
        lax.ppermute(owned, DP + TENSOR, toward_home(group, homes, step))
        for step in range(1, lax.axis_size(TENSOR))
    ]


def from_homes(group, homes, back):
    index, row = lax.axis_index(DP), lax.axis_index(TENSOR)
    received = jnp.where(row == home_row(index), back[0], jnp.zeros_like(back[0]))
    for step in range(1, lax.axis_size(TENSOR)):
        pairs = [(target, source) for source, target in toward_home(group, homes, step)]
        received = received + lax.ppermute(back[step], DP + TENSOR, pairs)
    return received


def from_columns(received):
    shape = (lax.axis_size(DP), -1, received.shape[1])
    return lax.all_to_all(received.reshape(shape), DP, split_axis=0, concat_axis=0, tiled=True)


FLIPPED = (False, False, False, True, False, False, True)
SHAPES = (
    (MODEL_WIDTH, QUERY_HEADS * HEAD_SIZE),
    (MODEL_WIDTH, KEY_VALUE_HEADS * HEAD_SIZE),
    (MODEL_WIDTH, KEY_VALUE_HEADS * HEAD_SIZE),
    (QUERY_HEADS * HEAD_SIZE, MODEL_WIDTH),
    (MODEL_WIDTH, FF),
    (MODEL_WIDTH, FF),
    (FF, MODEL_WIDTH),
)
FANS = (
    MODEL_WIDTH,
    MODEL_WIDTH,
    MODEL_WIDTH,
    QUERY_HEADS * HEAD_SIZE // 64,
    MODEL_WIDTH,
    MODEL_WIDTH,
    FF,
)


def advance_kernel(homes, *refs):
    late_ref, out_ref, gate_up_ref, down_ref = refs[:4]
    moment_refs, reduced_refs, fresh_refs = refs[4:11], refs[11:18], refs[18:25]
    slots_ref = refs[25]
    width_query, width_key = moment_refs[0].shape[1], moment_refs[1].shape[1]
    width_ff = moment_refs[4].shape[1]
    gradients = (
        late_ref[:, :width_query],
        late_ref[:, width_query : width_query + width_key],
        late_ref[:, width_query + width_key :],
        out_ref[...],
        gate_up_ref[:, :width_ff],
        gate_up_ref[:, width_ff:],
        down_ref[...],
    )
    slots_ref[...] = jnp.zeros_like(slots_ref)
    for number, gradient in enumerate(gradients):
        moment = moment_refs[number][...]
        if FLIPPED[number]:
            gradient_turned = gradient.T
            moment_next = MOMENTUM * moment + gradient_turned
            reduced_refs[number][...] = gradient_turned
            look = (gradient_turned + MOMENTUM * moment_next).T
        else:
            moment_next = MOMENTUM * moment + gradient
            reduced_refs[number][...] = gradient
            look = gradient + MOMENTUM * moment_next
        fresh_refs[number][...] = moment_next
        slots_ref[homes[number], :, : look.shape[1]] = look.astype(jnp.bfloat16)


def advance(sums, moments, homes, dp_count):
    rows = sums[0].shape[0]
    width = max(moment.shape[1] for moment in moments)
    shapes = [jax.ShapeDtypeStruct(moment.shape, jnp.float32) for moment in moments]
    results = in_vmem(
        functools.partial(advance_kernel, homes),
        list(sums) + list(moments),
        shapes + shapes + [jax.ShapeDtypeStruct((dp_count, rows, width), jnp.bfloat16)],
        [],
        0,
    )
    return results[:7], results[7:14], results[14]


def update_kernel(homes, *refs):
    returned_refs, refs = refs[:2], refs[2:]
    first = returned_refs[0].shape[2]
    for number in range(7):
        master_ref, result_ref = refs[number], refs[7 + number]
        width = master_ref.shape[0] if FLIPPED[number] else master_ref.shape[1]
        portion = returned_refs[0][homes[number], :, : min(width, first)]
        if width > first:
            rest = returned_refs[1][homes[number], :, : width - first]
            portion = jnp.concatenate([portion, rest], axis=1)
        portion = portion.astype(jnp.float32)
        if FLIPPED[number]:
            portion = portion.T
        step_size = 0.5 * FANS[number] ** (-0.5) * math.sqrt(max(SHAPES[number]))
        result_ref[...] = DECAY_KEEP * master_ref[...] - step_size * portion


def update(returned, masters, homes):
    return in_vmem(
        functools.partial(update_kernel, homes),
        list(returned) + list(masters),
        [jax.ShapeDtypeStruct(master.shape, jnp.float32) for master in masters],
        [],
        0,
    )


def on_device(
    hidden_in,
    out_grad,
    positions,
    query_weight,
    key_matrix,
    value_matrix,
    out_weight,
    gate_weight,
    up_weight,
    down_weight,
    query_moment,
    key_momentum,
    value_momentum,
    out_moment,
    gate_moment,
    up_moment,
    down_moment,
    gains,
    gain_first,
    gain_second,
):
    bf16 = jnp.bfloat16
    heads_local = jnp.concatenate(
        [query_weight.astype(bf16), key_matrix.astype(bf16), value_matrix.astype(bf16)], axis=1
    )
    out_local = out_weight.astype(bf16).T
    mlp_local = jnp.concatenate(
        [gate_weight.astype(bf16), up_weight.astype(bf16), down_weight.astype(bf16).T], axis=1
    )
    width_query = query_weight.shape[1]
    width_key = key_matrix.shape[1]
    width_ff = gate_weight.shape[1]
    heads_held = swap(both_cores(heads_local))
    hidden_in, positions, heads_held = tied(hidden_in, positions, heads_held)
    positions = swap(positions)
    hidden_in = swap(hidden_in)
    heads_near = gather_plane_near(heads_held)
    out_pair = both_cores(out_local)
    mlp_pair = both_cores(mlp_local)
    hidden_in, out_pair, heads_near = tied(hidden_in, out_pair, heads_near)
    heads_full = gather_plane_far(heads_near)
    out_held = swap(out_pair)
    gain_attn = gains[:MODEL_WIDTH]
    gain_mlp = gains[MODEL_WIDTH : 2 * MODEL_WIDTH]
    gain_query = gains[2 * MODEL_WIDTH : 2 * MODEL_WIDTH + HEAD_SIZE][None, :]
    gain_key = gains[2 * MODEL_WIDTH + HEAD_SIZE :][None, :]
    start = (jnp.arange(positions.shape[0], dtype=jnp.int32) - positions)[None, :]
    cosine_part, sine_part = rotary(positions)
    residual_in = hidden_in.astype(jnp.float32)
    normalized = rms_norm(residual_in, gain_attn).astype(jnp.bfloat16)

    attn_pair = gather_near(normalized, True)
    attn_pair, mlp_pair = tied(attn_pair, mlp_pair)
    mlp_held = swap(mlp_pair)
    attn_rows = gather_across(attn_pair, True)
    query, key, value, pre = project(
        attn_rows, heads_full, cosine_part, sine_part, gain_query, gain_key, width_query
    )
    query, out_held = tied(query, out_held)
    out_full = gather_plane_direct(out_held)
    mixed_heads, log_total = attend(query, key, value, start)
    mixed_heads, mlp_held = tied(mixed_heads, mlp_held)
    gate_up_near = gather_plane_near(mlp_held[:, : 2 * width_ff])
    down_held = mlp_held[:, 2 * width_ff :]
    saved = (query, key, value, pre, log_total)
    residual = residual_in + scatter_tokens(
        contract_cols(mixed_heads, out_full).astype(bf16), True
    )
    residual, down_held, out_grad = tied(residual, down_held, out_grad)
    out_grad = swap(out_grad)
    normed_mlp = rms_norm(residual, gain_mlp).astype(jnp.bfloat16)
    mlp_pair = gather_near(normed_mlp, False)
    mlp_pair, down_held, gate_up_near = tied(mlp_pair, down_held, gate_up_near)
    gate_up_full = gather_plane_far(gate_up_near)
    down_full = gather_plane(down_held)
    mlp_rows = gather_across(mlp_pair, False)
    cot_rows = gather_across(gather_near(out_grad, False), False)
    gate_up = matmul(mlp_rows, gate_up_full)
    gate_value = gate_up[:, :width_ff]
    up_value = gate_up[:, width_ff:]
    activated = (jax.nn.silu(gate_value) * up_value).astype(jnp.bfloat16)
    down_grad = contract_rows(cot_rows, activated).astype(bf16)
    cot_rows, down_grad = tied(cot_rows, down_grad)
    down_pieces = sum_plane(down_grad)
    d_activated = matmul(cot_rows, down_full)

    def swiglu(gate_in, up_in):
        return jax.nn.silu(gate_in) * up_in

    swiglu_out, swiglu_pull = jax.vjp(swiglu, gate_value, up_value)
    d_gate, d_up = swiglu_pull(d_activated)
    d_gate = d_gate.astype(jnp.bfloat16)
    d_up = d_up.astype(jnp.bfloat16)
    d_gate_up = jnp.concatenate([d_gate, d_up], axis=1)
    gate_up_grad = contract_rows(mlp_rows, d_gate_up)
    gate_up_pieces = sum_plane(gate_up_grad.astype(bf16))
    d_normed_mlp = scatter_tokens(contract_cols(d_gate_up, gate_up_full).astype(bf16), False)
    norm_out, norm_pull = jax.vjp(rms_norm, residual, gain_mlp)
    d_residual_norm, d_gain_mlp = norm_pull(d_normed_mlp)
    d_residual = out_grad.astype(jnp.float32) + d_residual_norm
    state_pair = gather_near(d_residual.astype(bf16), True)
    state_pair, down_pieces = tied(state_pair, down_pieces)
    state_rows = gather_across(state_pair, True)
    down_held = cross_sum(down_pieces)
    out_chunks = sum_far(contract_rows(state_rows, mixed_heads).astype(bf16))
    d_heads, d_gain_heads = attention_backward(
        state_rows, out_full, saved, cosine_part, sine_part, gain_query, gain_key, start
    )
    d_heads, gate_up_pieces, down_held, activated, out_chunks = tied(
        d_heads, gate_up_pieces, down_held, activated, out_chunks
    )
    block_part = contract_cols(activated, down_full).astype(bf16)
    gate_up_held = cross_sum(gate_up_pieces)
    out_pieces = sum_near(out_chunks)
    heads_grad = contract_rows(attn_rows, d_heads)
    late_chunks = sum_far(heads_grad.astype(bf16))
    late_chunks, out_pieces, d_heads = tied(late_chunks, out_pieces, d_heads)
    late_pieces = sum_near(late_chunks)
    out_held = cross_sum(out_pieces)
    late_pieces, gate_up_held, down_held, out_held = tied(
        late_pieces, gate_up_held, down_held, out_held
    )
    late_held = cross_sum(late_pieces)
    gate_up_sum = finish_sum(gate_up_held)
    down_sum = finish_sum(down_held)
    d_normed_pair = scatter_across(contract_cols(d_heads, heads_full).astype(bf16), True)
    block_pair = scatter_across(block_part, False)
    late_held, d_normed_pair, block_pair = tied(late_held, d_normed_pair, block_pair)
    late_sum = finish_sum(late_held)
    out_sum = finish_sum(out_held)
    d_normed = scatter_near(d_normed_pair, True)
    block_out = (residual + scatter_near(block_pair, False)).astype(bf16)
    masters = (
        query_weight,
        key_matrix,
        value_matrix,
        out_weight,
        gate_weight,
        up_weight,
        down_weight,
    )
    moments = (
        query_moment,
        key_momentum,
        value_momentum,
        out_moment,
        gate_moment,
        up_moment,
        down_moment,
    )
    homes = {4: 0, 5: 3, 6: 4, 0: 7, 3: 5, 1: 1, 2: 2}
    group = tuple(range(7))
    reduced, fresh, slots = advance(
        (late_sum, out_sum, gate_up_sum, down_sum), moments, homes, lax.axis_size(DP)
    )
    owned = to_columns(slots)
    owned, d_normed = tied(owned, d_normed)
    pieces = to_homes(group, homes, owned)
    input_out, input_pull = jax.vjp(rms_norm, residual_in, gain_attn)
    d_input_norm, d_gain_attn = input_pull(d_normed)
    input_grad = (d_residual + d_input_norm).astype(bf16)
    gain_grad = jnp.concatenate([d_gain_attn, d_gain_mlp, d_gain_heads.reshape(-1)])
    gain_grad = sum_everywhere(gain_grad, [(name, lax.axis_size(name)) for name in ("core", "pl")])
    both = jnp.concatenate([input_grad, block_out], axis=0)
    pieces, both, gain_grad = tied(pieces, both, gain_grad)
    back = orthogonalize(owns(group, homes), pieces)
    gain_grad = sum_everywhere(gain_grad, [("lo", lax.axis_size("lo"))])
    back, both, gain_grad = tied(back, both, gain_grad)
    back, both = tied(back, swap(both))
    half = len(back) // 2
    received = [from_homes(group, homes, part) for part in (back[:half], back[half:])]
    input_grad = half_of(both, 0).astype(jnp.float32)
    block_out = half_of(both, 1).astype(jnp.float32)
    received[1], gain_grad = tied(received[1], gain_grad)
    gain_grad = sum_everywhere(gain_grad, [("hi", 2)])
    updated = update([from_columns(part) for part in received], masters, homes)
    first_next = BETA_FIRST * gain_first + (1.0 - BETA_FIRST) * gain_grad
    second_next = BETA_SECOND * gain_second + (1.0 - BETA_SECOND) * gain_grad * gain_grad
    first_hat = first_next / (1.0 - BETA_FIRST**ADAM_STEP)
    second_hat = second_next / (1.0 - BETA_SECOND**ADAM_STEP)
    gains_next = gains - GAIN_RATE * first_hat / (jnp.sqrt(second_hat) + ADAM_EPS)
    return (
        block_out,
        input_grad,
        reduced[0],
        reduced[1],
        reduced[2],
        reduced[3],
        reduced[4],
        reduced[5],
        reduced[6],
        updated[0],
        updated[1],
        updated[2],
        updated[3],
        updated[4],
        updated[5],
        updated[6],
        fresh[0],
        fresh[1],
        fresh[2],
        fresh[3],
        fresh[4],
        fresh[5],
        fresh[6],
        first_next,
        second_next,
        gains_next,
    )


def solution(mesh):
    dp_count, tensor_count = mesh.shape["dp"], mesh.shape["tensor"]
    split = Mesh(
        mesh.devices.reshape(dp_count // 2, 2, 2, tensor_count // 2), ("pl", "core", "hi", "lo")
    )
    tokens = P(("pl", "core", "hi", "lo"), None)
    rows = P(DP, TENSOR)
    columns = P(TENSOR, DP)
    matrices = (rows, rows, rows, columns, rows, rows, columns)
    whole = (P(), P(), P())
    return jax.shard_map(
        on_device,
        mesh=split,
        in_specs=(tokens, tokens, P(DP)) + matrices + matrices + whole,
        out_specs=(tokens, tokens) + matrices + matrices + matrices + whole,
        check_vma=False,
    )
```

```python
import functools
import math

import jax
import jax.numpy as jnp
from jax import lax
from jax.experimental import pallas as pl
from jax.experimental.pallas import tpu as pltpu
from jax.sharding import Mesh, PartitionSpec as P

MODEL_WIDTH = 1024
QUERY_HEADS = 16
KEY_VALUE_HEADS = 8
HEAD_SIZE = 128
FF = 3072
NS_STEPS = 5
ADAM_STEP = 10


EPS_NORM = 1e-06
ROPE_BASE = 1000000.0
MASK_FILL = -1e30
MOMENTUM = 0.95
COEF_LINEAR = 3.4445
COEF_GRAM = -4.775
COEF_SQUARE = 2.0315
NS_EPS = 1e-07
DECAY_KEEP = 0.998
BETA_FIRST = 0.9
BETA_SECOND = 0.95
ADAM_EPS = 1e-08
GAIN_RATE = 0.6
ROW_BLOCK = 256


DP = ("pl", "core")
TENSOR = ("hi", "lo")


def matmul(left, right):
    return jnp.dot(left, right, preferred_element_type=jnp.float32)


def contract_rows(left, right):
    return lax.dot_general(
        left, right, (((0,), (0,)), ((), ())), preferred_element_type=jnp.float32
    )


def contract_cols(left, right):
    return lax.dot_general(
        left, right, (((1,), (1,)), ((), ())), preferred_element_type=jnp.float32
    )


def orthogonalize_kernel(owner_ref, *refs):
    count = (len(refs) - 4) // 3

    @pl.when(owner_ref[0] != 0)
    def _():
        orthogonalize_owned(count, refs)

    @pl.when(owner_ref[0] == 0)
    def _():
        for result in refs[count : 3 * count]:
            result[...] = jnp.zeros_like(result)


def orthogonalize_owned(count, refs):
    pieces, results = refs[:count], refs[count : 3 * count]
    current, gram, gram_low, mixing = refs[3 * count :]
    size, width = pieces[0].shape
    block = 256
    blocks = size // block
    for number, piece in enumerate(pieces):
        current[:, number * width : (number + 1) * width] = piece[...]
    diagonal = lax.broadcasted_iota(jnp.int32, (block, block), 0) == lax.broadcasted_iota(
        jnp.int32, (block, block), 1
    )

    def mix(number):
        for col in range(blocks):
            at = col * block
            gram[at:, at : at + block] = contract_cols(current[at:, :], current[at : at + block, :])
        trace = jnp.float32(0.0)
        for col in range(blocks):
            at = col * block
            trace += jnp.sum(jnp.where(diagonal, gram[at : at + block, at : at + block], 0.0))
        scale = jnp.where(number == 0, 1.0 / (jnp.sqrt(trace) + NS_EPS), 1.0)
        scale_square = scale * scale
        for col in range(blocks):
            at = col * block
            for row in range(col, blocks):
                to = row * block
                tile = gram[to : to + block, at : at + block] * scale_square
                gram[to : to + block, at : at + block] = tile
                gram_low[to : to + block, at : at + block] = tile.astype(jnp.bfloat16)
                if row > col:
                    gram_low[at : at + block, to : to + block] = tile.T.astype(jnp.bfloat16)
        for col in range(blocks):
            at = col * block
            square = matmul(gram_low[at:, :], gram_low[:, at : at + block])
            for row in range(col, blocks):
                to = row * block
                tile = COEF_GRAM * gram[to : to + block, at : at + block]
                tile += COEF_SQUARE * square[to - at : to - at + block]
                if row == col:
                    tile += jnp.where(diagonal, COEF_LINEAR, 0.0)
                tile = tile * scale
                mixing[to : to + block, at : at + block] = tile.astype(jnp.bfloat16)
                if row > col:
                    mixing[at : at + block, to : to + block] = tile.T.astype(jnp.bfloat16)

    def sweep(number, carry):
        mix(number)

        def columns(step, inner):
            span = pl.ds(pl.multiple_of(step * width, width), width)
            current[:, span] = matmul(mixing[...], current[:, span]).astype(jnp.bfloat16)
            return inner

        lax.fori_loop(0, count, columns, 0)
        return carry

    lax.fori_loop(0, NS_STEPS, sweep, 0)
    for number, result in enumerate(results):
        at = number % count * width
        if number < count:
            result[...] = current[:, at : at + result.shape[1]]
        else:
            result[...] = current[:, at + width - result.shape[1] : at + width]


def orthogonalize(owner, pieces):
    size, width = pieces[0].shape
    first = (width // 2 + 127) // 128 * 128
    total = width * len(pieces)
    flops = NS_STEPS * 2 * size * size * (total * 13 // 8 + size * 5 // 8)
    return pl.pallas_call(
        orthogonalize_kernel,
        out_shape=[
            jax.ShapeDtypeStruct((size, part), piece.dtype)
            for part in (first, width - first)
            for piece in pieces
        ],
        in_specs=[pl.BlockSpec(memory_space=pltpu.SMEM)]
        + [pl.BlockSpec(memory_space=pltpu.VMEM)] * len(pieces),
        out_specs=[pl.BlockSpec(memory_space=pltpu.VMEM)] * (2 * len(pieces)),
        scratch_shapes=[
            pltpu.VMEM((size, total), jnp.bfloat16),
            pltpu.VMEM((size, size), jnp.float32),
            pltpu.VMEM((size, size), jnp.bfloat16),
            pltpu.VMEM((size, size), jnp.bfloat16),
        ],
        compiler_params=pltpu.CompilerParams(vmem_limit_bytes=48 * 1024 * 1024),
        cost_estimate=pl.CostEstimate(
            flops=flops, bytes_accessed=4 * size * total, transcendentals=0
        ),
    )(owner.astype(jnp.int32).reshape(1), *pieces)


def tied(*values):
    return lax.optimization_barrier(values)


def swap(values):
    return lax.ppermute(values, ("core", "hi"), [(0, 0), (1, 2), (2, 1), (3, 3)])


def to_partner(values, name):
    return lax.ppermute(values, name, [(0, 1), (1, 0)])


def in_order(first, mine, theirs):
    return jnp.concatenate([jnp.where(first, mine, theirs), jnp.where(first, theirs, mine)], axis=0)


def half_of(values, which):
    rows = values.shape[0] // 2
    return lax.dynamic_slice_in_dim(values, which * rows, rows, 0)


def gather_near(values, ordered):
    if lax.axis_size("lo") == 2:
        other = to_partner(values, "lo")
        if ordered:
            return in_order(lax.axis_index("lo") == 0, values, other)
        return jnp.concatenate([values, other], axis=0)
    return lax.all_gather(values, "lo", axis=0, tiled=True)


def gather_across(pair, ordered):
    other = to_partner(pair, "core")
    if ordered:
        return in_order(lax.axis_index("core") == 0, pair, other)
    return jnp.concatenate([pair, other], axis=0)


def scatter_across(values, ordered):
    place = lax.axis_index("core") if ordered else 0
    received = to_partner(half_of(values, 1 - place), "core").astype(jnp.float32)
    return half_of(values, place).astype(jnp.float32) + received


def scatter_near(pair, ordered):
    if lax.axis_size("lo") == 2:
        place = lax.axis_index("lo") if ordered else 0
        received = to_partner(half_of(pair, 1 - place).astype(jnp.bfloat16), "lo")
        return half_of(pair, place) + received.astype(jnp.float32)
    return lax.psum_scatter(
        pair.astype(jnp.bfloat16), "lo", scatter_dimension=0, tiled=True
    ).astype(jnp.float32)


def scatter_tokens(values, ordered):
    return scatter_near(scatter_across(values, ordered), ordered)


def both_cores(shard):
    return in_order(lax.axis_index("core") == 0, shard, to_partner(shard, "core"))


def exchange(values, stride):
    count = lax.axis_size("pl")
    return lax.ppermute(values, "pl", [(index, index ^ stride) for index in range(count)])


def in_places(found, held):
    rows = held.shape[0] * lax.axis_size("pl")
    full = jnp.zeros((rows, held.shape[1]), held.dtype)
    for piece, at in found:
        full = lax.dynamic_update_slice_in_dim(full, piece, at, 0)
    return full


def gather_plane_direct(held):
    place = lax.axis_index("pl")
    rows = held.shape[0]
    found = [(held, place * rows)]
    for stride in range(1, lax.axis_size("pl")):
        found.append((exchange(held, stride), (place ^ stride) * rows))
    return in_places(found, held)


def gather_plane_near(held):
    if lax.axis_size("pl") != 4:
        return [held] + [exchange(held, stride) for stride in range(1, lax.axis_size("pl"))]
    return [held, exchange(held, 1), exchange(held, 2)]


def gather_plane_far(near):
    place = lax.axis_index("pl")
    rows = near[0].shape[0]
    half = rows // 2
    found = [(piece, (place ^ stride) * rows) for stride, piece in enumerate(near)]
    if lax.axis_size("pl") == 4:
        found.append((exchange(near[2][:half], 1), (place ^ 3) * rows))
        found.append((exchange(near[1][half:], 2), (place ^ 3) * rows + half))
    return in_places(found, near[0])


def gather_plane(held):
    return gather_plane_far(gather_plane_near(held))


def sum_far(values):
    count = lax.axis_size("pl")
    place = lax.axis_index("pl")
    rows = values.shape[0] // count
    half = rows // 2
    chunks = [
        lax.dynamic_slice_in_dim(values, (place ^ stride) * rows, rows, 0) for stride in range(count)
    ]
    if count != 4:
        return chunks
    return chunks[:3] + [exchange(chunks[3][half:], 2), exchange(chunks[3][:half], 1)]


def sum_near(chunks):
    count = lax.axis_size("pl")
    if count != 4:
        return chunks[:1] + [exchange(chunks[stride], stride) for stride in range(1, count)]
    mine, first, second, for_first, for_second = chunks
    half = mine.shape[0] // 2
    first = jnp.concatenate([first[:half], add(first[half:], for_first)], axis=0)
    second = jnp.concatenate([add(second[:half], for_second), second[half:]], axis=0)
    return [mine, exchange(first, 1), exchange(second, 2)]


def sum_plane(values):
    return sum_near(sum_far(values))


def add(left, right):
    return (left.astype(jnp.float32) + right.astype(jnp.float32)).astype(jnp.bfloat16)


def cross_sum(pieces):
    total = sum(piece.astype(jnp.float32) for piece in pieces)
    return swap(total.astype(jnp.bfloat16))


def finish_sum(held):
    place = lax.axis_index("core")
    received = to_partner(half_of(held, 1 - place), "core")
    return half_of(held, place).astype(jnp.float32) + received.astype(jnp.float32)


def sum_everywhere(values, sizes):
    for name, count in sizes:
        stride = 1
        while stride < count:
            pairs = [(index, index ^ stride) for index in range(count)]
            values = values + lax.ppermute(values, name, pairs)
            stride *= 2
    return values


def rms_norm(values, gain):
    return values * lax.rsqrt(jnp.mean(values * values, axis=-1, keepdims=True) + EPS_NORM) * gain


def rotary(positions):
    half_width = HEAD_SIZE // 2
    inverse = jnp.power(
        jnp.float32(ROPE_BASE), -(jnp.arange(half_width, dtype=jnp.float32) * (2.0 / HEAD_SIZE))
    )
    angles = positions.astype(jnp.float32)[:, None] * inverse[None, :]
    cosine_part = jnp.cos(angles)
    sine_part = jnp.sin(angles)
    return (
        jnp.concatenate([cosine_part, cosine_part], axis=-1),
        jnp.concatenate([-sine_part, sine_part], axis=-1),
    )


def visible_pairs(start_ref, block, extent, rows):
    query = block * rows + lax.broadcasted_iota(jnp.int32, (extent, rows), 1)
    key = lax.broadcasted_iota(jnp.int32, (extent, rows), 0)
    begin = start_ref[:, block * rows : (block + 1) * rows]
    return (key <= query) & (key >= begin)


def turn_half(values):
    return pltpu.roll(values, HEAD_SIZE // 2, 1)


def project_kernel(
    rows_ref,
    weight_ref,
    cosine_ref,
    sine_ref,
    gain_query_ref,
    gain_key_ref,
    query_ref,
    key_ref,
    value_ref,
    pre_ref,
):
    total_rows = rows_ref.shape[0]
    width_query, width_key = query_ref.shape[1], key_ref.shape[1]
    size = ROW_BLOCK
    low = jnp.bfloat16

    def project(block, carry):
        span = pl.ds(pl.multiple_of(block * size, size), size)
        pre = matmul(rows_ref[span, :], weight_ref[...])
        pre_ref[span, :] = pre[:, : width_query + width_key]
        cosine, sine = cosine_ref[span, :], sine_ref[span, :]
        for at in range(0, width_query + width_key, HEAD_SIZE):
            gain_ref = gain_query_ref if at < width_query else gain_key_ref
            normal = rms_norm(pre[:, at : at + HEAD_SIZE], gain_ref[...])
            turned = (normal * cosine + turn_half(normal) * sine).astype(low)
            if at < width_query:
                query_ref[span, at : at + HEAD_SIZE] = turned
            else:
                key_ref[span, at - width_query : at - width_query + HEAD_SIZE] = turned
        value_ref[span, :] = pre[:, width_query + width_key :].astype(low)
        return carry

    lax.fori_loop(0, total_rows // size, project, 0)


def attend_kernel(
    query_ref, key_ref, value_ref, start_ref, mixed_ref, log_total_ref, turned_value
):
    total_rows = query_ref.shape[0]
    width_query, width_key = query_ref.shape[1], key_ref.shape[1]
    size = ROW_BLOCK
    scale = HEAD_SIZE**-0.5
    low = jnp.bfloat16

    def prepare(block, carry):
        span = pl.ds(pl.multiple_of(block * size, size), size)
        for at in range(0, width_key, HEAD_SIZE):
            value = value_ref[span, at : at + HEAD_SIZE].astype(jnp.float32)
            turned_value[at : at + HEAD_SIZE, span] = value.T.astype(low)
        return carry

    lax.fori_loop(0, total_rows // size, prepare, 0)
    group = width_query // width_key
    for block in range(total_rows // size):
        extent = (block + 1) * size
        rows = slice(block * size, extent)
        visible = visible_pairs(start_ref, block, extent, size)
        for head in range(width_query // HEAD_SIZE):
            key_at = head // group * HEAD_SIZE
            lanes = slice(head * HEAD_SIZE, (head + 1) * HEAD_SIZE)
            key_lanes = slice(key_at, key_at + HEAD_SIZE)
            scores = contract_cols(key_ref[:extent, key_lanes], query_ref[rows, lanes])
            scores = jnp.where(visible, scores, MASK_FILL)
            row_max = jnp.max(scores, axis=0, keepdims=True)
            weights = jnp.exp((scores - row_max) * scale)
            total = jnp.sum(weights, axis=0, keepdims=True)
            log_total_ref[head : head + 1, rows] = row_max * scale + jnp.log(total)
            weights = (weights * (1.0 / total)).astype(low)
            mixed = matmul(turned_value[key_lanes, :extent], weights)
            mixed_ref[rows, lanes] = mixed.T.astype(low)


def attention_backward_kernel(
    state_ref,
    out_ref,
    query_ref,
    key_ref,
    value_ref,
    pre_ref,
    log_total_ref,
    cosine_ref,
    sine_ref,
    gain_query_ref,
    gain_key_ref,
    start_ref,
    d_heads_ref,
    d_gain_ref,
    d_mixed,
    turned_key,
    d_query,
    d_key,
    d_value,
):
    total_rows = state_ref.shape[0]
    width_query, width_key = query_ref.shape[1], key_ref.shape[1]
    size = ROW_BLOCK
    scale = HEAD_SIZE**-0.5
    low = jnp.bfloat16

    def prepare(block, carry):
        span = pl.ds(pl.multiple_of(block * size, size), size)
        d_mixed[span, :] = matmul(state_ref[span, :], out_ref[...]).astype(low)
        for at in range(0, width_key, HEAD_SIZE):
            key = key_ref[span, at : at + HEAD_SIZE].astype(jnp.float32)
            turned_key[at : at + HEAD_SIZE, span] = key.T.astype(low)
        return carry

    lax.fori_loop(0, total_rows // size, prepare, 0)
    d_key[...] = jnp.zeros_like(d_key)
    d_value[...] = jnp.zeros_like(d_value)
    group = width_query // width_key
    for block in range(total_rows // size):
        extent = (block + 1) * size
        rows = slice(block * size, extent)
        visible = visible_pairs(start_ref, block, extent, size)
        for head in range(width_query // HEAD_SIZE):
            key_at = head // group * HEAD_SIZE
            lanes = slice(head * HEAD_SIZE, (head + 1) * HEAD_SIZE)
            key_lanes = slice(key_at, key_at + HEAD_SIZE)
            query = query_ref[rows, lanes]
            cotangent = d_mixed[rows, lanes]
            scores = contract_cols(key_ref[:extent, key_lanes], query) * scale
            probs = jnp.exp(scores - log_total_ref[head : head + 1, rows])
            probs = jnp.where(visible, probs, 0.0)
            d_probs = contract_cols(value_ref[:extent, key_lanes], cotangent)
            shift = jnp.sum(d_probs * probs, axis=0, keepdims=True)
            d_scores = (probs * (d_probs - shift)).astype(low)
            d_value[:extent, key_lanes] += matmul(probs.astype(low), cotangent)
            d_key[:extent, key_lanes] += matmul(d_scores, query)
            d_query[rows, lanes] = matmul(turned_key[key_lanes, :extent], d_scores).T * scale

    def finish(block, carry):
        span = pl.ds(pl.multiple_of(block * size, size), size)
        cosine, sine = cosine_ref[span, :], sine_ref[span, :]
        sums = []
        for at in range(0, width_query + width_key, HEAD_SIZE):
            if at < width_query:
                gain, cotangent = gain_query_ref[...], d_query[span, at : at + HEAD_SIZE]
            else:
                begin = at - width_query
                gain = gain_key_ref[...]
                cotangent = d_key[span, begin : begin + HEAD_SIZE] * scale
            cotangent = cotangent * cosine - turn_half(cotangent) * sine
            pre = pre_ref[span, at : at + HEAD_SIZE]
            inverse = lax.rsqrt(jnp.mean(pre * pre, axis=-1, keepdims=True) + EPS_NORM)
            normal = pre * inverse
            sums.append(jnp.sum(cotangent * normal, axis=0, keepdims=True))
            pulled = cotangent * gain
            inner = jnp.mean(normal * pulled, axis=-1, keepdims=True)
            d_pre = inverse * (pulled - normal * inner)
            d_heads_ref[span, at : at + HEAD_SIZE] = d_pre.astype(low)
        d_heads_ref[span, width_query + width_key :] = d_value[span, :].astype(low)
        heads_query = width_query // HEAD_SIZE
        return carry[0] + sum(sums[:heads_query]), carry[1] + sum(sums[heads_query:])

    zero = jnp.zeros((1, HEAD_SIZE), jnp.float32)
    for_query, for_key = lax.fori_loop(0, total_rows // size, finish, (zero, zero))
    d_gain_ref[0:1, :] = for_query
    d_gain_ref[1:2, :] = for_key


def in_vmem(kernel, operands, results, scratch, flops):
    moved = sum(math.prod(item.shape) * item.dtype.itemsize for item in operands + results)
    return pl.pallas_call(
        kernel,
        out_shape=results,
        in_specs=[pl.BlockSpec(memory_space=pltpu.VMEM)] * len(operands),
        out_specs=[pl.BlockSpec(memory_space=pltpu.VMEM)] * len(results),
        scratch_shapes=scratch,
        compiler_params=pltpu.CompilerParams(vmem_limit_bytes=48 * 1024 * 1024),
        cost_estimate=pl.CostEstimate(flops=flops, bytes_accessed=moved, transcendentals=0),
    )(*operands)


def project(rows, weight, cosine, sine, gain_query, gain_key, width_query):
    total_rows, columns = rows.shape
    width_key = (weight.shape[1] - width_query) // 2
    low = jnp.bfloat16
    shape = jax.ShapeDtypeStruct
    return in_vmem(
        project_kernel,
        [rows, weight, cosine, sine, gain_query, gain_key],
        [
            shape((total_rows, width_query), low),
            shape((total_rows, width_key), low),
            shape((total_rows, width_key), low),
            shape((total_rows, width_query + width_key), jnp.float32),
        ],
        [],
        2 * total_rows * columns * weight.shape[1],
    )


def attend(query, key, value, start):
    total_rows, width_query = query.shape
    width_key = key.shape[1]
    shape = jax.ShapeDtypeStruct
    return in_vmem(
        attend_kernel,
        [query, key, value, start],
        [
            shape((total_rows, width_query), jnp.bfloat16),
            shape((width_query // HEAD_SIZE, total_rows), jnp.float32),
        ],
        [pltpu.VMEM((width_key, total_rows), jnp.bfloat16)],
        4 * total_rows * total_rows * width_query,
    )


def attention_backward(
    state, out_full, saved, cosine, sine, gain_query, gain_key, start
):
    query, key, value, pre, log_total = saved
    total_rows, columns = state.shape
    width_query, width_key = query.shape[1], key.shape[1]
    low = jnp.bfloat16
    shape = jax.ShapeDtypeStruct
    return in_vmem(
        attention_backward_kernel,
        [state, out_full, query, key, value, pre, log_total]
        + [cosine, sine, gain_query, gain_key, start],
        [
            shape((total_rows, width_query + 2 * width_key), low),
            shape((2, HEAD_SIZE), jnp.float32),
        ],
        [
            pltpu.VMEM((total_rows, width_query), low),
            pltpu.VMEM((width_key, total_rows), low),
            pltpu.VMEM((total_rows, width_query), jnp.float32),
            pltpu.VMEM((total_rows, width_key), jnp.float32),
            pltpu.VMEM((total_rows, width_key), jnp.float32),
        ],
        2 * total_rows * columns * width_query + 10 * total_rows * total_rows * width_query,
    )


def home_row(index):
    return lax.axis_size(TENSOR) // 2 - 1 + index % 2


def owns(group, homes):
    index, row = lax.axis_index(DP), lax.axis_index(TENSOR)
    mine = functools.reduce(jnp.logical_or, [index == homes[number] for number in group])
    return mine & (row == home_row(index))


def toward_home(group, homes, step):
    rows = lax.axis_size(TENSOR)
    return [
        (index * rows + (home_row(index) + step) % rows, index * rows + home_row(index))
        for index in sorted(homes[number] for number in group)
    ]


def to_columns(slots):
    owned = lax.all_to_all(slots, DP, split_axis=0, concat_axis=0, tiled=True)
    return owned.reshape(-1, slots.shape[2])


def to_homes(group, homes, owned):
    return [owned] + [
        lax.ppermute(owned, DP + TENSOR, toward_home(group, homes, step))
        for step in range(1, lax.axis_size(TENSOR))
    ]


def from_homes(group, homes, back):
    index, row = lax.axis_index(DP), lax.axis_index(TENSOR)
    received = jnp.where(row == home_row(index), back[0], jnp.zeros_like(back[0]))
    for step in range(1, lax.axis_size(TENSOR)):
        pairs = [(target, source) for source, target in toward_home(group, homes, step)]
        received = received + lax.ppermute(back[step], DP + TENSOR, pairs)
    return received


def from_columns(received):
    shape = (lax.axis_size(DP), -1, received.shape[1])
    return lax.all_to_all(received.reshape(shape), DP, split_axis=0, concat_axis=0, tiled=True)


FLIPPED = (False, False, False, True, False, False, True)
SHAPES = (
    (MODEL_WIDTH, QUERY_HEADS * HEAD_SIZE),
    (MODEL_WIDTH, KEY_VALUE_HEADS * HEAD_SIZE),
    (MODEL_WIDTH, KEY_VALUE_HEADS * HEAD_SIZE),
    (QUERY_HEADS * HEAD_SIZE, MODEL_WIDTH),
    (MODEL_WIDTH, FF),
    (MODEL_WIDTH, FF),
    (FF, MODEL_WIDTH),
)
FANS = (
    MODEL_WIDTH,
    MODEL_WIDTH,
    MODEL_WIDTH,
    QUERY_HEADS * HEAD_SIZE // 64,
    MODEL_WIDTH,
    MODEL_WIDTH,
    FF,
)


def advance_kernel(homes, *refs):
    late_ref, out_ref, gate_up_ref, down_ref = refs[:4]
    moment_refs, reduced_refs, fresh_refs = refs[4:11], refs[11:18], refs[18:25]
    slots_ref = refs[25]
    width_query, width_key = moment_refs[0].shape[1], moment_refs[1].shape[1]
    width_ff = moment_refs[4].shape[1]
    gradients = (
        late_ref[:, :width_query],
        late_ref[:, width_query : width_query + width_key],
        late_ref[:, width_query + width_key :],
        out_ref[...],
        gate_up_ref[:, :width_ff],
        gate_up_ref[:, width_ff:],
        down_ref[...],
    )
    slots_ref[...] = jnp.zeros_like(slots_ref)
    for number, gradient in enumerate(gradients):
        moment = moment_refs[number][...]
        if FLIPPED[number]:
            gradient_turned = gradient.T
            moment_next = MOMENTUM * moment + gradient_turned
            reduced_refs[number][...] = gradient_turned
            look = (gradient_turned + MOMENTUM * moment_next).T
        else:
            moment_next = MOMENTUM * moment + gradient
            reduced_refs[number][...] = gradient
            look = gradient + MOMENTUM * moment_next
        fresh_refs[number][...] = moment_next
        slots_ref[homes[number], :, : look.shape[1]] = look.astype(jnp.bfloat16)


def advance(sums, moments, homes, dp_count):
    rows = sums[0].shape[0]
    width = max(moment.shape[1] for moment in moments)
    shapes = [jax.ShapeDtypeStruct(moment.shape, jnp.float32) for moment in moments]
    results = in_vmem(
        functools.partial(advance_kernel, homes),
        list(sums) + list(moments),
        shapes + shapes + [jax.ShapeDtypeStruct((dp_count, rows, width), jnp.bfloat16)],
        [],
        0,
    )
    return results[:7], results[7:14], results[14]


def update_kernel(homes, *refs):
    returned_refs, refs = refs[:2], refs[2:]
    first = returned_refs[0].shape[2]
    for number in range(7):
        master_ref, result_ref = refs[number], refs[7 + number]
        width = master_ref.shape[0] if FLIPPED[number] else master_ref.shape[1]
        portion = returned_refs[0][homes[number], :, : min(width, first)]
        if width > first:
            rest = returned_refs[1][homes[number], :, : width - first]
            portion = jnp.concatenate([portion, rest], axis=1)
        portion = portion.astype(jnp.float32)
        if FLIPPED[number]:
            portion = portion.T
        step_size = 0.5 * FANS[number] ** (-0.5) * math.sqrt(max(SHAPES[number]))
        result_ref[...] = DECAY_KEEP * master_ref[...] - step_size * portion


def update(returned, masters, homes):
    return in_vmem(
        functools.partial(update_kernel, homes),
        list(returned) + list(masters),
        [jax.ShapeDtypeStruct(master.shape, jnp.float32) for master in masters],
        [],
        0,
    )


def on_device(
    hidden_in,
    out_grad,
    positions,
    query_weight,
    key_matrix,
    value_matrix,
    out_weight,
    gate_weight,
    up_weight,
    down_weight,
    query_moment,
    key_momentum,
    value_momentum,
    out_moment,
    gate_moment,
    up_moment,
    down_moment,
    gains,
    gain_first,
    gain_second,
):
    bf16 = jnp.bfloat16
    heads_local = jnp.concatenate(
        [query_weight.astype(bf16), key_matrix.astype(bf16), value_matrix.astype(bf16)], axis=1
    )
    out_local = out_weight.astype(bf16).T
    mlp_local = jnp.concatenate(
        [gate_weight.astype(bf16), up_weight.astype(bf16), down_weight.astype(bf16).T], axis=1
    )
    width_query = query_weight.shape[1]
    width_key = key_matrix.shape[1]
    width_ff = gate_weight.shape[1]
    heads_held = swap(both_cores(heads_local))
    hidden_in, positions, heads_held = tied(hidden_in, positions, heads_held)
    positions = swap(positions)
    hidden_in = swap(hidden_in)
    heads_near = gather_plane_near(heads_held)
    out_pair = both_cores(out_local)
    mlp_pair = both_cores(mlp_local)
    hidden_in, positions, out_pair, heads_near = tied(hidden_in, positions, out_pair, heads_near)
    heads_full = gather_plane_far(heads_near)
    out_held = swap(out_pair)
    gain_attn = gains[:MODEL_WIDTH]
    gain_mlp = gains[MODEL_WIDTH : 2 * MODEL_WIDTH]
    gain_query = gains[2 * MODEL_WIDTH : 2 * MODEL_WIDTH + HEAD_SIZE][None, :]
    gain_key = gains[2 * MODEL_WIDTH + HEAD_SIZE :][None, :]
    start = (jnp.arange(positions.shape[0], dtype=jnp.int32) - positions)[None, :]
    cosine_part, sine_part = rotary(positions)
    residual_in = hidden_in.astype(jnp.float32)
    normalized = rms_norm(residual_in, gain_attn).astype(jnp.bfloat16)

    attn_pair = gather_near(normalized, True)
    attn_pair, mlp_pair = tied(attn_pair, mlp_pair)
    mlp_held = swap(mlp_pair)
    attn_rows = gather_across(attn_pair, True)
    query, key, value, pre = project(
        attn_rows, heads_full, cosine_part, sine_part, gain_query, gain_key, width_query
    )
    query, out_held = tied(query, out_held)
    out_full = gather_plane_direct(out_held)
    mixed_heads, log_total = attend(query, key, value, start)
    mixed_heads, mlp_held = tied(mixed_heads, mlp_held)
    gate_up_near = gather_plane_near(mlp_held[:, : 2 * width_ff])
    down_held = mlp_held[:, 2 * width_ff :]
    saved = (query, key, value, pre, log_total)
    residual = residual_in + scatter_tokens(
        contract_cols(mixed_heads, out_full).astype(bf16), True
    )
    residual, down_held, out_grad = tied(residual, down_held, out_grad)
    out_grad = swap(out_grad)
    normed_mlp = rms_norm(residual, gain_mlp).astype(jnp.bfloat16)
    mlp_pair = gather_near(normed_mlp, False)
    mlp_pair, down_held, gate_up_near = tied(mlp_pair, down_held, gate_up_near)
    gate_up_full = gather_plane_far(gate_up_near)
    down_full = gather_plane(down_held)
    mlp_rows = gather_across(mlp_pair, False)
    cot_rows = gather_across(gather_near(out_grad, False), False)
    gate_up = matmul(mlp_rows, gate_up_full)
    gate_value = gate_up[:, :width_ff]
    up_value = gate_up[:, width_ff:]
    activated = (jax.nn.silu(gate_value) * up_value).astype(jnp.bfloat16)
    down_grad = contract_rows(cot_rows, activated).astype(bf16)
    cot_rows, down_grad = tied(cot_rows, down_grad)
    down_pieces = sum_plane(down_grad)
    d_activated = matmul(cot_rows, down_full)

    def swiglu(gate_in, up_in):
        return jax.nn.silu(gate_in) * up_in

    swiglu_out, swiglu_pull = jax.vjp(swiglu, gate_value, up_value)
    d_gate, d_up = swiglu_pull(d_activated)
    d_gate = d_gate.astype(jnp.bfloat16)
    d_up = d_up.astype(jnp.bfloat16)
    d_gate_up = jnp.concatenate([d_gate, d_up], axis=1)
    gate_up_grad = contract_rows(mlp_rows, d_gate_up)
    gate_up_pieces = sum_plane(gate_up_grad.astype(bf16))
    d_normed_mlp = scatter_tokens(contract_cols(d_gate_up, gate_up_full).astype(bf16), False)
    norm_out, norm_pull = jax.vjp(rms_norm, residual, gain_mlp)
    d_residual_norm, d_gain_mlp = norm_pull(d_normed_mlp)
    d_residual = out_grad.astype(jnp.float32) + d_residual_norm
    state_pair = gather_near(d_residual.astype(bf16), True)
    state_pair, down_pieces = tied(state_pair, down_pieces)
    state_rows = gather_across(state_pair, True)
    down_held = cross_sum(down_pieces)
    out_chunks = sum_far(contract_rows(state_rows, mixed_heads).astype(bf16))
    d_heads, d_gain_heads = attention_backward(
        state_rows, out_full, saved, cosine_part, sine_part, gain_query, gain_key, start
    )
    d_heads, gate_up_pieces, down_held, activated, out_chunks = tied(
        d_heads, gate_up_pieces, down_held, activated, out_chunks
    )
    block_part = contract_cols(activated, down_full).astype(bf16)
    gate_up_held = cross_sum(gate_up_pieces)
    out_pieces = sum_near(out_chunks)
    heads_grad = contract_rows(attn_rows, d_heads)
    late_chunks = sum_far(heads_grad.astype(bf16))
    late_chunks, out_pieces, d_heads = tied(late_chunks, out_pieces, d_heads)
    late_pieces = sum_near(late_chunks)
    out_held = cross_sum(out_pieces)
    late_pieces, gate_up_held, down_held, out_held = tied(
        late_pieces, gate_up_held, down_held, out_held
    )
    late_held = cross_sum(late_pieces)
    gate_up_sum = finish_sum(gate_up_held)
    down_sum = finish_sum(down_held)
    d_normed_pair = scatter_across(contract_cols(d_heads, heads_full).astype(bf16), True)
    block_pair = scatter_across(block_part, False)
    late_held, d_normed_pair, block_pair = tied(late_held, d_normed_pair, block_pair)
    late_sum = finish_sum(late_held)
    out_sum = finish_sum(out_held)
    d_normed = scatter_near(d_normed_pair, True)
    block_out = (residual + scatter_near(block_pair, False)).astype(bf16)
    masters = (
        query_weight,
        key_matrix,
        value_matrix,
        out_weight,
        gate_weight,
        up_weight,
        down_weight,
    )
    moments = (
        query_moment,
        key_momentum,
        value_momentum,
        out_moment,
        gate_moment,
        up_moment,
        down_moment,
    )
    homes = {4: 0, 5: 3, 6: 4, 0: 7, 3: 5, 1: 1, 2: 2}
    group = tuple(range(7))
    reduced, fresh, slots = advance(
        (late_sum, out_sum, gate_up_sum, down_sum), moments, homes, lax.axis_size(DP)
    )
    owned = to_columns(slots)
    owned, d_normed = tied(owned, d_normed)
    pieces = to_homes(group, homes, owned)
    input_out, input_pull = jax.vjp(rms_norm, residual_in, gain_attn)
    d_input_norm, d_gain_attn = input_pull(d_normed)
    input_grad = (d_residual + d_input_norm).astype(bf16)
    gain_grad = jnp.concatenate([d_gain_attn, d_gain_mlp, d_gain_heads.reshape(-1)])
    gain_grad = sum_everywhere(gain_grad, [(name, lax.axis_size(name)) for name in ("core", "pl")])
    both = jnp.concatenate([input_grad, block_out], axis=0)
    pieces, both, gain_grad = tied(pieces, both, gain_grad)
    back = orthogonalize(owns(group, homes), pieces)
    gain_grad = sum_everywhere(gain_grad, [("lo", lax.axis_size("lo"))])
    back, both, gain_grad = tied(back, both, gain_grad)
    back, both = tied(back, swap(both))
    half = len(back) // 2
    received = [from_homes(group, homes, part) for part in (back[:half], back[half:])]
    input_grad = half_of(both, 0).astype(jnp.float32)
    block_out = half_of(both, 1).astype(jnp.float32)
    received[1], gain_grad = tied(received[1], gain_grad)
    gain_grad = sum_everywhere(gain_grad, [("hi", 2)])
    updated = update([from_columns(part) for part in received], masters, homes)
    first_next = BETA_FIRST * gain_first + (1.0 - BETA_FIRST) * gain_grad
    second_next = BETA_SECOND * gain_second + (1.0 - BETA_SECOND) * gain_grad * gain_grad
    first_hat = first_next / (1.0 - BETA_FIRST**ADAM_STEP)
    second_hat = second_next / (1.0 - BETA_SECOND**ADAM_STEP)
    gains_next = gains - GAIN_RATE * first_hat / (jnp.sqrt(second_hat) + ADAM_EPS)
    return (
        block_out,
        input_grad,
        reduced[0],
        reduced[1],
        reduced[2],
        reduced[3],
        reduced[4],
        reduced[5],
        reduced[6],
        updated[0],
        updated[1],
        updated[2],
        updated[3],
        updated[4],
        updated[5],
        updated[6],
        fresh[0],
        fresh[1],
        fresh[2],
        fresh[3],
        fresh[4],
        fresh[5],
        fresh[6],
        first_next,
        second_next,
        gains_next,
    )


def solution(mesh):
    dp_count, tensor_count = mesh.shape["dp"], mesh.shape["tensor"]
    split = Mesh(
        mesh.devices.reshape(dp_count // 2, 2, 2, tensor_count // 2), ("pl", "core", "hi", "lo")
    )
    tokens = P(("pl", "core", "hi", "lo"), None)
    rows = P(DP, TENSOR)
    columns = P(TENSOR, DP)
    matrices = (rows, rows, rows, columns, rows, rows, columns)
    whole = (P(), P(), P())
    return jax.shard_map(
        on_device,
        mesh=split,
        in_specs=(tokens, tokens, P(DP)) + matrices + matrices + whole,
        out_specs=(tokens, tokens) + matrices + matrices + matrices + whole,
        check_vma=False,
    )
```
